512 devices in a mesh: grp: 2 (over y_lo), space: 64 (over z, x), mem: 4 (over y_hi, core).
Axes of the slice: x: 4, y: 4 (y_hi: 2, y_lo: 2; y = y_hi * 2 + y_lo), z: 16, core: 2. Of those that a mesh axis runs over, the one named last changes fastest.
Arguments:
- start_field: float32 [4, 1024, 32, 256], P('mem', 'space', 'grp'), may hold values from -6 to 6
- material: int32 [1024, 32, 256], P('space', 'grp'), may hold values from 0 to 7
- conductivity: float32 [4, 8], P('mem'), may hold values from 0.02 to 0.16
- owners: int32 [4, 2, 64, 128, 1], P('mem', 'grp'), may hold values from 0 to 63; in each aligned block of 128 rows (0 to 127, 128 to 255, ..., all dimensions but the last counted through in order) at most 4 rows name the same one
- tile_ids: int32 [4, 2, 64, 128], P('mem', 'grp'), may hold values from 0 to 15
- embed_weight: bfloat16 [512, 1536], P(None, ('grp', 'mem')), may hold values from -0.25 to 0.25
- layer_norm_gain: float32 [1536], replicated, may hold values from 0.5 to 1.5
- w_qkv: bfloat16 [3, 1536, 1024], P(None, None, ('grp', 'mem')), may hold values from -1.5 to 1.5
- w_out: bfloat16 [1024, 1536], P(('grp', 'mem')), may hold values from -0.1875 to 0.1875
- w_read: bfloat16 [1536, 128], replicated, may hold values from -0.15625 to 0.15625
Outputs:
- final_field: float32 [4, 1024, 32, 256], P('mem', 'space', 'grp')
- grad_qkv: bfloat16 [3, 1536, 1024], P(None, None, ('grp', 'mem'))
- grad_gain: float32 [1536], replicated
The draws below stay inside these ranges and needn't reach their ends.
Inputs may be any that keep to these rules, and one draw needn't show every extreme that they name: `owners`: in each aligned block of 128 rows (the slots of one member, half and shard) no owner is named more than 4 times, and in some blocks one owner exactly 4 times.
All inputs are finite; a program needn't handle non-finite values.
Results may differ from the reference program's by a relative error of at most 0.015.
Values may be sent and summed in bfloat16 or wider, within the bound.
No kernel may reach another device: no remote copies, remote signals or barrier semaphores. Data moves between devices by JAX's collectives and lax.ppermute only.
A program may use at most 64 MiB of HBM per device.

```python
import math
import jax
import jax.numpy as jnp
import numpy as np
from jax import lax

CX = 16
CY = 16
CZ = 256
SPD = 128
STEPS = 3
TILE = 16
MATS = 8
D = 1536
HEADS = 8
HD = 128
MEMBERS = 4
NX = 1024
NY = 32
NZ = 256
HK = 1024
TOKV = 512
TGT = 128
CAP = 4
ROWS = 1024
TILES_DEV = 16
N_GRP = 2
N_SPACE = 64


def draw_w_qkv(key, part):
    key = jax.random.fold_in(key, 7)
    normal_base = jax.random.normal(key, (3, D, HK), jnp.float32)
    return jnp.clip(normal_base / math.sqrt(D), -0.15, 0.15).astype(jnp.bfloat16)


def with_ends(drawn, rng, low, largest):
    longest = drawn.shape.index(max(drawn.shape))
    spots = []
    for shift in (0, 1):
        where = [jax.random.randint(jax.random.fold_in(rng, axis), (), 0, length) for axis, length in enumerate(drawn.shape)]
        where[longest] = (where[longest] + shift) % drawn.shape[longest]
        spots.append(tuple(where))
    return drawn.at[spots[0]].set(low).at[spots[1]].set(largest)


def block_scale(own_key, dims, cuts, low, top_value):
    def one(position, blocks):
        heights = jax.random.uniform(jax.random.fold_in(jax.random.fold_in(own_key, 6), position), (blocks,), jnp.float32, low / len(cuts), top_value / len(cuts))
        return jnp.repeat(jnp.exp(heights), dims[position] // blocks).reshape((-1,) + (1,) * (len(dims) - position - 1))

    level = one(*cuts[0])
    for cut in cuts[1:]:
        level = level * one(*cut)
    return level


def deal_out(rng, own, number, rows, number_of, top, reach, skew):
    ranking = jax.random.permutation(rng, number_of)
    crowded, usual = load_shares(number_of, rows * top, reach, skew, True), load_shares(number_of, rows * top, reach, skew, False)
    places = jnp.arange(number_of)

    def named(sizes, rotation):
        used = int((sizes > 0).sum())
        fixed = max(1, used // 4)
        shifted = fixed + (places - fixed + rotation * (used - fixed)) % max(1, number_of - fixed)
        return jnp.zeros((number_of,), jnp.int32).at[ranking[jnp.where(places < fixed, places, shifted)]].set(jnp.asarray(sizes, jnp.int32))

    sizes = jnp.where(number % 4 == 0, named(crowded, number // 4), named(usual, number - number // 4 - 1))
    mixed = jax.random.permutation(jax.random.fold_in(own, 3), number_of)
    donor, sink = mixed[0:number_of // 2 * 2:2], mixed[1:number_of // 2 * 2:2]
    room = jnp.minimum(sizes[donor] - 1, reach - sizes[sink]) // 2
    room = jnp.where((donor == ranking[0]) | (sink == ranking[0]) | (sizes[sink] == 0), 0, jnp.maximum(room, 0))
    shifted = jax.random.randint(jax.random.fold_in(own, 4), (number_of // 2,), 0, 1 << 20) % (room + 1)
    sizes = sizes.at[donor].add(-shifted).at[sink].add(shifted)
    labels = jnp.searchsorted(jnp.cumsum(sizes), jnp.arange(rows * top), side="right").astype(jnp.int32)
    listing = labels.reshape(top, rows).T
    listing = listing[jax.random.permutation(jax.random.fold_in(own, 1), rows)]
    rotation = jax.random.randint(jax.random.fold_in(own, 2), (rows, 1), 0, top)
    return jnp.take_along_axis(listing, (jnp.arange(top)[None, :] + rotation) % top, axis=1)


def load_shares(count, total, bound, slope, full):
    weights = [(1 << 20) // math.isqrt(rank ** slope) + 1 for rank in range(1, count + 1)]
    largest = bound if full else min(bound, max(-(-total // count), total * weights[0] // sum(weights)))
    least = 1 if total - largest >= count - 1 else 0
    holding, rest = [largest] + [least] * (count - 1), total - largest - least * (count - 1)
    while rest > 0:
        movable = [i for i in range(1, count) if holding[i] < largest] or [i for i in range(1, count) if holding[i] < bound]
        whole, remaining = sum([weights[i] for i in movable]), rest
        for i in movable:
            addition = min(bound - holding[i], max(1, remaining * weights[i] // whole), rest)
            holding[i] = holding[i] + addition
            rest = rest - addition
    return np.array(holding)


def bell_draw(stream_key, extent, scale, most, cuts=(), held_as=jnp.bfloat16):
    values = scale * jax.random.normal(stream_key, extent, jnp.float32)
    if cuts:
        values = values * block_scale(stream_key, extent, cuts, -0.22, 0.18)
    return jnp.clip(values, -most, most).astype(held_as)


def setup_inputs(seed: int = 0) -> dict:
    streams_of = jax.random.split(jax.random.key(seed), 11)
    start_field = bell_draw(streams_of[0], (MEMBERS, NX, NY, NZ), 1.0, 6.0, ((0, 4), (1, 64), (2, 2)), jnp.float32)
    material = with_ends(jax.random.randint(streams_of[1], (NX, NY, NZ), 0, MATS), jax.random.fold_in(streams_of[1], 1), 0, MATS - 1).astype(jnp.int32)
    conductivity = jnp.clip(jnp.exp(math.log(0.16) - 2.0794415 * jax.random.uniform(streams_of[2], (MEMBERS, MATS), jnp.float32) ** block_scale(streams_of[2], (MEMBERS, MATS), ((0, 4),), -0.2, 0.2)), 0.02, 0.16)
    owners_keys = jax.random.split(jax.random.fold_in(streams_of[3], 1), MEMBERS * N_GRP * N_SPACE * SPD // SPD)
    owners_turns = jax.random.permutation(jax.random.fold_in(streams_of[3], 3), MEMBERS * N_GRP * N_SPACE * SPD // SPD)
    owners = jax.vmap(lambda own, number: deal_out(jax.random.fold_in(streams_of[3], 2), own, number, SPD, N_SPACE, 1, CAP, 2))(owners_keys, owners_turns).reshape((MEMBERS, N_GRP, N_SPACE, SPD, 1))
    tile_ids = with_ends(jax.random.randint(streams_of[4], (MEMBERS, N_GRP, N_SPACE, SPD), 0, TILES_DEV), jax.random.fold_in(streams_of[4], 1), 0, TILES_DEV - 1).astype(jnp.int32)
    embed_weight = bell_draw(streams_of[5], (TOKV, D), TOKV ** -0.5, 0.25, ((1, 8),))
    layer_norm_gain = jnp.clip(1.0 + 0.1 * jax.random.normal(streams_of[6], (D,), jnp.float32), 0.5, 1.5)
    w_qkv = draw_w_qkv(jax.random.fold_in(streams_of[10], 71), 0)
    w_out = bell_draw(streams_of[8], (HK, D), HK ** -0.5, 0.1875, ((0, 8),))
    w_read = bell_draw(streams_of[9], (D, TGT), D ** -0.5, 0.15625)
    return {"start_field": start_field, "material": material, "conductivity": conductivity, "owners": owners, "tile_ids": tile_ids, "embed_weight": embed_weight, "layer_norm_gain": layer_norm_gain, "w_qkv": w_qkv, "w_out": w_out, "w_read": w_read}


NORM_EPSILON = 1e-06

def reduced_precision(values):
    return lax.optimization_barrier(values.astype(jnp.bfloat16))

def conduct(material, table_row):
    conductance = jnp.zeros(material.shape, jnp.float32)
    for level_id in range(MATS):
        conductance = conductance + jnp.where(material == level_id, table_row[level_id], jnp.float32(0.0))
    return conductance

def relax_step(padded_field, padded_cond):
    field_ext = jnp.pad(padded_field, ((0, 0), (0, 0), (1, 1)))
    cond_ext = jnp.pad(padded_cond, ((0, 0), (0, 0), (1, 1)))
    center = field_ext[1:-1, 1:-1, 1:-1]
    center_cond = cond_ext[1:-1, 1:-1, 1:-1]
    change = jnp.zeros_like(center)
    for axis_id in range(3):
        for offset in (0, 2):
            window = [slice(1, 1 + center.shape[0]), slice(1, 1 + center.shape[1]), slice(1, 1 + center.shape[2])]
            window[axis_id] = slice(offset, offset + center.shape[axis_id])
            window = tuple(window)
            change = change + 0.5 * (center_cond + cond_ext[window]) * (field_ext[window] - center)
    return center + change

def tiles_of(field):
    shaped = field.reshape(N_SPACE, CX // TILE, TILE, N_GRP, CY // TILE, TILE, CZ // TILE, TILE)
    shaped = shaped.transpose(0, 3, 1, 4, 6, 2, 5, 7)
    return shaped.reshape(N_SPACE, N_GRP, TILES_DEV, TILE, TILE, TILE)

def coarse_tokens(tiles):
    leading = tiles.shape[:-3]
    shaped = tiles.reshape(leading + (TILE // 2, 2, TILE // 2, 2, TILE // 2, 2))
    return lax.optimization_barrier(jnp.mean(shaped, axis=(-5, -3, -1))).reshape(leading + (TOKV,))

def coarse_targets(tiles):
    leading = tiles.shape[:-3]
    shaped = tiles.reshape(leading + (TILE // 4, 4, TILE // 4, 4, TILE // 2, 2))
    return lax.optimization_barrier(jnp.mean(shaped, axis=(-5, -3, -1))).reshape(leading + (TGT,))

def reference(start_field, material, conductivity, owners, tile_ids, embed_weight, layer_norm_gain, w_qkv, w_out, w_read):
    final_list = []
    token_list = []
    target_list = []
    margin = ((1, 1), (1, 1), (0, 0))
    for member in range(MEMBERS):
        conductance = conduct(material, conductivity[member])
        cond_pad = jnp.pad(conductance, margin)
        current = start_field[member]
        before_last = current
        for section_id in range(STEPS):
            before_last = current
            current = relax_step(jnp.pad(current, margin), cond_pad)
        final_list.append(current)
        token_list.append(reduced_precision(coarse_tokens(tiles_of(before_last))))
        target_list.append(reduced_precision(coarse_targets(tiles_of(current))))
    token_all = jnp.stack(token_list)
    target_all = jnp.stack(target_list)
    member_index = jnp.arange(MEMBERS, dtype=jnp.int32)[:, None, None, None]
    half_index = jnp.arange(N_GRP, dtype=jnp.int32)[None, :, None, None]
    owner_index = owners[..., 0].astype(jnp.int32)
    tile_index = tile_ids.astype(jnp.int32)
    chosen_tokens = token_all[member_index, owner_index, half_index, tile_index]
    chosen_targets = target_all[member_index, owner_index, half_index, tile_index]
    shard_tokens = chosen_tokens.transpose(2, 1, 0, 3, 4).reshape(N_SPACE, ROWS, TOKV)
    shard_targets = chosen_targets.transpose(2, 1, 0, 3, 4).reshape(N_SPACE, ROWS, TGT)
    score_scale = 1.0 / math.sqrt(HD)
    loss_scale = math.sqrt(D / (N_SPACE * ROWS * TGT))
    seq_count = ROWS // SPD
    qkv_wide = w_qkv.astype(jnp.float32)
    read_wide = w_read.astype(jnp.float32)

    def shard_step(carry, batch_pair):
        tokens, targets = batch_pair
        embedded = reduced_precision(jnp.dot(tokens, embed_weight, preferred_element_type=jnp.float32))
        embedded_wide = embedded.astype(jnp.float32)
        row_mean = lax.optimization_barrier(jnp.mean(embedded_wide, axis=1, keepdims=True))
        mean_removed = embedded_wide - row_mean
        row_variance = lax.optimization_barrier(jnp.mean(mean_removed * mean_removed, axis=1, keepdims=True))
        standardized_input = mean_removed * lax.rsqrt(row_variance + NORM_EPSILON)
        normalized_rows = reduced_precision(standardized_input * layer_norm_gain)
        projected = reduced_precision(jnp.einsum('rd,tdc->trc', normalized_rows.astype(jnp.float32), qkv_wide))
        split_heads = projected.astype(jnp.float32).reshape(3, seq_count, SPD, HEADS, HD)
        query_rows, key_rows, value_rows = (split_heads[0], split_heads[1], split_heads[2])
        scores = jnp.einsum('bqhd,bkhd->bhqk', query_rows, key_rows) * score_scale
        top_score = lax.optimization_barrier(jnp.max(scores, axis=-1, keepdims=True))
        raised = jnp.exp(scores - top_score)
        prob_table = raised / lax.optimization_barrier(jnp.sum(raised, axis=-1, keepdims=True))
        probs_low = reduced_precision(prob_table).astype(jnp.float32)
        attended = jnp.einsum('bhqk,bkhd->bqhd', probs_low, value_rows).astype(jnp.bfloat16).reshape(ROWS, HK)
        mixed = jnp.dot(attended, w_out, preferred_element_type=jnp.float32)
        prediction = jnp.dot(embedded_wide + mixed, read_wide, precision=lax.Precision.HIGHEST)
        delta = (prediction - targets.astype(jnp.float32)) * loss_scale
        upstream = reduced_precision(jnp.dot(delta, read_wide.T, precision=lax.Precision.HIGHEST))
        grad_attended = reduced_precision(jnp.dot(upstream, w_out.T, preferred_element_type=jnp.float32))
        grad_attended = grad_attended.astype(jnp.float32).reshape(seq_count, SPD, HEADS, HD)
        grad_probs = jnp.einsum('bqhd,bkhd->bhqk', grad_attended, value_rows)
        grad_values = reduced_precision(jnp.einsum('bhqk,bqhd->bkhd', probs_low, grad_attended)).astype(jnp.float32)
        inner_sum = lax.optimization_barrier(jnp.sum(prob_table * grad_probs, axis=-1, keepdims=True))
        grad_scores = reduced_precision(prob_table * (grad_probs - inner_sum) * score_scale).astype(jnp.float32)
        grad_queries = reduced_precision(jnp.einsum('bhqk,bkhd->bqhd', grad_scores, key_rows)).astype(jnp.float32)
        grad_keys = reduced_precision(jnp.einsum('bhqk,bqhd->bkhd', grad_scores, query_rows)).astype(jnp.float32)
        grad_proj = jnp.stack([grad_queries, grad_keys, grad_values]).reshape(3, ROWS, HK)
        grad_weights = jnp.einsum('rd,trc->tdc', normalized_rows.astype(jnp.float32), grad_proj)
        gradient_normalized = jnp.einsum('trc,tdc->rd', grad_proj, qkv_wide)
        gain_contribution = lax.optimization_barrier(jnp.sum(gradient_normalized * standardized_input, axis=0))
        return ((carry[0] + grad_weights, carry[1] + gain_contribution), None)
    zero_init = (jnp.zeros((3, D, HK), jnp.float32), jnp.zeros((D,), jnp.float32))
    totals, unused = lax.scan(shard_step, zero_init, (shard_tokens, shard_targets))
    return (jnp.stack(final_list), totals[0].astype(jnp.bfloat16), totals[1])
```

```python
import math

import jax
import jax.numpy as jnp
from jax import lax
from jax.sharding import Mesh
from jax.sharding import PartitionSpec as P

SPD = 128
STEPS = 3
TILE = 16
HD = 128
NORM_EPSILON = 1e-06

SPACE = ("z", "x")
MEM = ("yhi", "core")
GROUP = ("grp", "yhi", "core")


def material_cond(material, table_row):
    conductance = jnp.zeros(material.shape, jnp.float32)
    for level_id in range(table_row.shape[0]):
        conductance = conductance + jnp.where(
            material == level_id, table_row[level_id], jnp.float32(0.0)
        )
    return conductance


def with_halo(block, width):
    half = lax.axis_index("grp")
    face = jnp.where(half == 0, block[:, :, -width:], block[:, :, :width])
    got = lax.ppermute(face, "grp", [(0, 1), (1, 0)])
    low = jnp.where(half == 0, 0.0, got)
    high = jnp.where(half == 0, got, 0.0)
    block = jnp.concatenate([low, block, high], axis=2)
    count = lax.axis_size(SPACE)
    forward = [(i, i + 1) for i in range(count - 1)]
    backward = [(i + 1, i) for i in range(count - 1)]
    low = lax.ppermute(block[:, -width:], SPACE, forward)
    high = lax.ppermute(block[:, :width], SPACE, backward)
    return jnp.concatenate([low, block, high], axis=1)


def relax_step(field, cond, inside):
    field_ext = jnp.pad(field, ((0, 0), (0, 0), (1, 1)))
    cond_ext = jnp.pad(cond, ((0, 0), (0, 0), (1, 1)))
    center = field_ext[1:-1, 1:-1, 1:-1]
    center_cond = cond_ext[1:-1, 1:-1, 1:-1]
    change = jnp.zeros_like(center)
    for axis_id in range(3):
        for offset in (0, 2):
            window = [slice(1, 1 + size) for size in center.shape]
            window[axis_id] = slice(offset, offset + center.shape[axis_id])
            window = tuple(window)
            change = change + 0.5 * (center_cond + cond_ext[window]) * (field_ext[window] - center)
    return jnp.where(inside, center + change, 0.0)


def solve_slab(field, conductance):
    span_x, span_y = field.shape[:2]
    padded = with_halo(jnp.stack([field, conductance]), STEPS)
    place_x = lax.axis_index(SPACE) * span_x
    place_y = lax.axis_index("grp") * span_y
    total_x = lax.axis_size(SPACE) * span_x
    total_y = lax.axis_size("grp") * span_y
    current, cond = padded[0], padded[1]
    for step in range(STEPS):
        before_last = current
        edge = STEPS - 1 - step
        row = place_x - edge + jnp.arange(span_x + 2 * edge)
        col = place_y - edge + jnp.arange(span_y + 2 * edge)
        inside = ((row >= 0) & (row < total_x))[:, None, None] & (
            (col >= 0) & (col < total_y)
        )[None, :, None]
        current = relax_step(current, cond, inside)
        cond = cond[1:-1, 1:-1]
    return before_last[1:-1, 1:-1], current


def cut_tiles(field, tile_size):
    span_x, span_y, span_z = field.shape
    shaped = field.reshape(
        span_x // tile_size,
        tile_size,
        span_y // tile_size,
        tile_size,
        span_z // tile_size,
        tile_size,
    )
    return shaped.transpose(0, 2, 4, 1, 3, 5).reshape(-1, tile_size, tile_size, tile_size)


def coarse_tokens(tiles, tile_size):
    count_tiles = tiles.shape[0]
    half_size = tile_size // 2
    shaped = tiles.reshape(count_tiles, half_size, 2, half_size, 2, half_size, 2)
    return jnp.mean(shaped, axis=(2, 4, 6)).reshape(count_tiles, -1)


def coarse_targets(tiles, tile_size):
    count_tiles = tiles.shape[0]
    shaped = tiles.reshape(count_tiles, tile_size // 4, 4, tile_size // 4, 4, tile_size // 2, 2)
    return jnp.mean(shaped, axis=(2, 4, 6)).reshape(count_tiles, -1)


def swap(parts, axis):
    return lax.all_to_all(parts, axis, split_axis=0, concat_axis=0, tiled=True)


def spread(own, axis):
    count = lax.axis_size(axis)
    return swap(jnp.broadcast_to(own[None], (count,) + own.shape), axis)


def relay_samples(rows, owner_list, tile_list):
    slot_count = owner_list.shape[1]
    capacity = 2 * slot_count // lax.axis_size(SPACE)
    my_index = lax.axis_index(SPACE)
    same_owner = owner_list[:, :, None] == owner_list[:, None, :]
    slot_order = jnp.arange(slot_count, dtype=jnp.int32)
    earlier = slot_order[None, :] < slot_order[:, None]
    slot_rank = jnp.sum((same_owner & earlier[None]).astype(jnp.int32), axis=2)
    owned_here = owner_list == my_index
    slot_ids = jnp.arange(capacity, dtype=jnp.int32)
    slot_match = owned_here[:, None, :] & (slot_rank[:, None, :] == slot_ids[None, :, None])
    chosen = jnp.sum(jnp.where(slot_match, tile_list[:, None, :] + 1, 0), axis=2) - 1
    present = (chosen >= 0)[:, :, None]
    picked = jnp.maximum(chosen, 0)
    send = jnp.where(present, rows[picked], jnp.zeros((), jnp.bfloat16))
    got = swap(send, SPACE)
    own_owner = jnp.take(owner_list, my_index, axis=0)
    own_rank = jnp.take(slot_rank, my_index, axis=0)
    flat_index = own_owner * capacity + own_rank
    return got.reshape(-1, got.shape[2])[flat_index]


def sum_over_space(grads):
    count_x, count_z = lax.axis_size("x"), lax.axis_size("z")
    columns = grads.shape[-1]
    parts = grads.astype(jnp.bfloat16).reshape(count_x, -1, columns)
    part = jnp.sum(swap(parts, "x").astype(jnp.float32), axis=0)
    parts = part.astype(jnp.bfloat16).reshape(count_z, -1, columns)
    total = jnp.sum(swap(parts, "z").astype(jnp.float32), axis=0).astype(jnp.bfloat16)
    whole = spread(total, "z").reshape(-1, columns)
    return spread(whole, "x").reshape(grads.shape)


def train_shard(samples, targets, embed_weight, layer_norm_gain, w_qkv, w_out, w_read):
    part_index = lax.axis_index(GROUP)
    embed_full = lax.all_gather(embed_weight, GROUP, axis=1, tiled=True)
    mixing = jnp.dot(w_out, w_read, preferred_element_type=jnp.float32)
    mixing_high = mixing.astype(jnp.bfloat16)
    mixing_low = (mixing - mixing_high.astype(jnp.float32)).astype(jnp.bfloat16)
    mixing_pair = jnp.concatenate([mixing_high, mixing_low], axis=0)

    tokens = spread(samples, GROUP).reshape(-1, samples.shape[1])
    row_count = tokens.shape[0]
    embedded = jnp.dot(tokens, embed_full, preferred_element_type=jnp.float32).astype(jnp.bfloat16)
    embedded_wide = embedded.astype(jnp.float32)
    row_mean = jnp.mean(embedded_wide, axis=1, keepdims=True)
    mean_removed = embedded_wide - row_mean
    row_variance = jnp.mean(mean_removed * mean_removed, axis=1, keepdims=True)
    standardized_input = mean_removed * lax.rsqrt(row_variance + NORM_EPSILON)
    normalized_rows = (standardized_input * layer_norm_gain).astype(jnp.bfloat16)
    projected = jnp.einsum(
        "rd,tdc->trc", normalized_rows, w_qkv, preferred_element_type=jnp.float32
    ).astype(jnp.bfloat16)
    seq_count = row_count // SPD
    query_rows, key_rows, value_rows = projected.reshape(3, seq_count, SPD, HD)
    score_scale = 1.0 / math.sqrt(HD)
    scores = (
        jnp.einsum("bqd,bkd->bqk", query_rows, key_rows, preferred_element_type=jnp.float32)
        * score_scale
    )
    top_score = jnp.max(scores, axis=-1, keepdims=True)
    raised = jnp.exp(scores - top_score)
    prob_table = raised / jnp.sum(raised, axis=-1, keepdims=True)
    probs_low = prob_table.astype(jnp.bfloat16)
    attended = jnp.einsum("bqk,bkd->bqd", probs_low, value_rows, preferred_element_type=jnp.float32)
    attended = attended.astype(jnp.bfloat16).reshape(row_count, HD)
    partial_pred = jnp.dot(
        jnp.concatenate([attended, attended], axis=1),
        mixing_pair,
        preferred_element_type=jnp.float32,
    )
    shares = swap(partial_pred.astype(jnp.bfloat16).reshape(seq_count, SPD, -1), GROUP)
    own_rows = lax.dynamic_slice_in_dim(embedded, part_index * SPD, SPD, 0)
    prediction = jnp.sum(shares.astype(jnp.float32), axis=0) + jnp.dot(
        own_rows, w_read, preferred_element_type=jnp.float32
    )
    loss_scale = math.sqrt(
        w_read.shape[0] / (lax.axis_size(SPACE) * row_count * w_read.shape[1])
    )
    own_delta = ((prediction - targets.astype(jnp.float32)) * loss_scale).astype(jnp.bfloat16)
    delta = spread(own_delta, GROUP).reshape(row_count, -1)
    mixing_t = jnp.concatenate([mixing_high, mixing_low], axis=1).T
    grad_attended = jnp.dot(
        jnp.concatenate([delta, delta], axis=1), mixing_t, preferred_element_type=jnp.float32
    ).astype(jnp.bfloat16)
    grad_attended = grad_attended.reshape(seq_count, SPD, HD)
    grad_probs = jnp.einsum(
        "bqd,bkd->bqk", grad_attended, value_rows, preferred_element_type=jnp.float32
    )
    grad_values = jnp.einsum(
        "bqk,bqd->bkd", probs_low, grad_attended, preferred_element_type=jnp.float32
    ).astype(jnp.bfloat16)
    inner_sum = jnp.sum(prob_table * grad_probs, axis=-1, keepdims=True)
    grad_scores = (prob_table * (grad_probs - inner_sum) * score_scale).astype(jnp.bfloat16)
    grad_queries = jnp.einsum(
        "bqk,bkd->bqd", grad_scores, key_rows, preferred_element_type=jnp.float32
    ).astype(jnp.bfloat16)
    grad_keys = jnp.einsum(
        "bqk,bqd->bkd", grad_scores, query_rows, preferred_element_type=jnp.float32
    ).astype(jnp.bfloat16)
    grad_proj = jnp.stack([grad_queries, grad_keys, grad_values]).reshape(3, row_count, HD)
    grad_weights = jnp.einsum(
        "rd,trc->tdc", normalized_rows, grad_proj, preferred_element_type=jnp.float32
    )
    weight_total = sum_over_space(grad_weights)
    gain_share = (
        jnp.sum(w_qkv.astype(jnp.float32) * weight_total.astype(jnp.float32), axis=(0, 2))
        / layer_norm_gain
    )
    gain_total = jnp.sum(spread(gain_share, GROUP), axis=0)
    return (weight_total, gain_total)


def shards(
    start_field,
    material,
    conductivity,
    owners,
    tile_ids,
    embed_weight,
    layer_norm_gain,
    w_qkv,
    w_out,
    w_read,
):
    conductance = material_cond(material, conductivity[0])
    before_last, final_local = solve_slab(start_field[0], conductance)
    token_rows = coarse_tokens(cut_tiles(before_last, TILE), TILE).astype(jnp.bfloat16)
    target_rows = coarse_targets(cut_tiles(final_local, TILE), TILE).astype(jnp.bfloat16)
    rows = jnp.concatenate([token_rows, target_rows], axis=1)
    samples = relay_samples(rows, owners[0, 0, :, :, 0], tile_ids[0, 0])
    width = token_rows.shape[1]
    grad_weights, grad_gain = train_shard(
        samples[:, :width],
        samples[:, width:],
        embed_weight,
        layer_norm_gain,
        w_qkv,
        w_out,
        w_read,
    )
    return (final_local[None], grad_weights, grad_gain)


def solution(mesh):
    halves, space, members = (mesh.shape[name] for name in ("grp", "space", "mem"))
    fine = Mesh(
        mesh.devices.reshape(halves, space // 4, 4, members // 2, 2),
        ("grp", "z", "x", "yhi", "core"),
    )
    placed = (
        P(MEM, SPACE, "grp", None),
        P(SPACE, "grp", None),
        P(MEM, None),
        P(MEM, "grp", None, None, None),
        P(MEM, "grp", None, None),
        P(None, GROUP),
        P(),
        P(None, None, GROUP),
        P(GROUP, None),
        P(),
    )
    return jax.shard_map(
        shards,
        mesh=fine,
        in_specs=placed,
        out_specs=(P(MEM, SPACE, "grp", None), P(None, None, GROUP), P()),
        check_vma=False,
    )
```

```python
import functools
import math

import jax
import jax.numpy as jnp
from jax import lax
from jax.experimental import pallas as pl
from jax.experimental.pallas import tpu as pltpu
from jax.sharding import Mesh
from jax.sharding import PartitionSpec as P

SPD = 128
STEPS = 3
TILE = 16
HD = 128
NORM_EPSILON = 1e-06

SPACE = ("z", "x")
MEM = ("yhi", "core")
GROUP = ("grp", "yhi", "core")
CHIPS = ("grp", "yhi")

PAD = 8
BLOCK_ROWS = 256
VMEM = pl.BlockSpec(memory_space=pltpu.VMEM)
SMEM = pl.BlockSpec(memory_space=pltpu.SMEM)
LIMIT = 48 * 1024 * 1024
EXACT = lax.Precision.HIGHEST


def swap(parts, axis):
    return lax.all_to_all(parts, axis, split_axis=0, concat_axis=0, tiled=True)


def spread(own, axis):
    count = lax.axis_size(axis)
    return swap(jnp.broadcast_to(own[None], (count,) + own.shape), axis)


def swap_cores(own):
    return lax.ppermute(own, "core", [(0, 1), (1, 0)])


def halos(block, width):
    half = lax.axis_index("grp")
    face = jnp.where(half == 0, block[:, :, -width:], block[:, :, :width])
    side = lax.ppermute(face, "grp", [(0, 1), (1, 0)])
    count = lax.axis_size(SPACE)
    forward = [(i, i + 1) for i in range(count - 1)]
    backward = [(i + 1, i) for i in range(count - 1)]
    top = jnp.concatenate([side[:, -width:], block[:, -width:], side[:, -width:]], axis=2)
    bottom = jnp.concatenate([side[:, :width], block[:, :width], side[:, :width]], axis=2)
    low = lax.ppermute(top, SPACE, forward)
    high = lax.ppermute(bottom, SPACE, backward)
    return side, low, high


def slab_kernel(
    place_ref,
    table_ref,
    field_ref,
    material_ref,
    side_ref,
    low_ref,
    high_ref,
    pick_ref,
    final_ref,
    send_ref,
    field_a,
    field_b,
    cond,
    coef,
    pairs,
    quads,
    rows_t,
    *,
    total_x,
    total_y,
):
    span_x, span_y, span_z = field_ref.shape
    width = low_ref.shape[1]
    rows = span_y + 2 * PAD
    planes = span_x + 2 * width
    own_x = slice(width, width + span_x)
    own_y = slice(PAD, PAD + span_y)
    ext_y = slice(PAD - width, PAD + span_y + width)

    field_a[...] = jnp.zeros_like(field_a)
    cond[...] = jnp.zeros_like(cond)
    for part, target in ((0, field_a), (1, cond)):
        target[own_x, slice(PAD - width, PAD), :] = side_ref[part]
        target[own_x, slice(PAD + span_y, PAD + span_y + width), :] = side_ref[part]
        target[slice(0, width), ext_y, :] = low_ref[part]
        target[slice(width + span_x, planes), ext_y, :] = high_ref[part]
    field_a[own_x, own_y, :] = field_ref[...]
    cond[own_x, own_y, :] = material_ref[...].astype(jnp.float32)

    place_x = place_ref[0] * span_x - width
    place_y = place_ref[1] * span_y - PAD
    row_id = place_y + lax.broadcasted_iota(jnp.int32, (rows, span_z), 0)
    col_id = lax.broadcasted_iota(jnp.int32, (rows, span_z), 1)
    inside_y = (row_id >= 0) & (row_id < total_y)
    first_z = col_id == 0
    last_z = col_id == span_z - 1

    def inside(plane):
        at = place_x + plane
        in_x = ((at >= 0) & (at < total_x)).astype(jnp.int32)
        return inside_y & (jnp.full((rows, span_z), in_x) > 0)

    def set_cond(plane, _):
        kind = cond[plane]
        value = jnp.zeros_like(kind)
        for level in range(table_ref.shape[0]):
            value = jnp.where(kind == float(level), table_ref[level], value)
        keep = inside(plane)
        cond[plane] = jnp.where(keep, value, 0.0)
        field_a[plane] = jnp.where(keep, field_a[plane], 0.0)
        return 0

    lax.fori_loop(0, planes, set_cond, 0)

    def set_coef(plane, _):
        mine = 0.5 * cond[plane]
        keep = inside(plane)
        ups = mine + pltpu.roll(mine, 1, 0)
        downs = mine + pltpu.roll(mine, rows - 1, 0)
        before = mine + jnp.where(first_z, 0.0, pltpu.roll(mine, 1, 1))
        after = mine + jnp.where(last_z, 0.0, pltpu.roll(mine, span_z - 1, 1))
        left = mine + 0.5 * cond[plane - 1]
        right = mine + 0.5 * cond[plane + 1]
        rest = 1.0 - (ups + downs + before + after + left + right)
        coef[0, plane] = jnp.where(keep, rest, 0.0)
        coef[1, plane] = jnp.where(keep, left, 0.0)
        coef[2, plane] = jnp.where(keep, right, 0.0)
        coef[3, plane] = jnp.where(keep, ups, 0.0)
        coef[4, plane] = jnp.where(keep, downs, 0.0)
        coef[5, plane] = jnp.where(keep & ~first_z, before, 0.0)
        coef[6, plane] = jnp.where(keep & ~last_z, after, 0.0)
        return 0

    lax.fori_loop(1, planes - 1, set_coef, 0)

    def step(source, target):
        def one(plane, _):
            mid = source[plane]
            value = coef[0, plane] * mid
            value = value + coef[1, plane] * source[plane - 1]
            value = value + coef[2, plane] * source[plane + 1]
            value = value + coef[3, plane] * pltpu.roll(mid, 1, 0)
            value = value + coef[4, plane] * pltpu.roll(mid, rows - 1, 0)
            value = value + coef[5, plane] * pltpu.roll(mid, 1, 1)
            value = value + coef[6, plane] * pltpu.roll(mid, span_z - 1, 1)
            target[plane] = value
            return 0

        return one

    for number in range(STEPS):
        source, target = (field_a, field_b) if number % 2 == 0 else (field_b, field_a)
        lax.fori_loop(1 + number, planes - 1 - number, step(source, target), 0)

    before_last, last = (field_a, field_b) if STEPS % 2 == 1 else (field_b, field_a)
    final_ref[...] = last[own_x, own_y, :]

    for i in range(span_x // 2):
        plane = width + 2 * i
        pairs[span_y * i : span_y * (i + 1), :] = (
            before_last[plane, own_y, :] + before_last[plane + 1, own_y, :]
        )
    for i in range(span_x // 4):
        plane = width + 4 * i
        quads[span_y * i : span_y * (i + 1), :] = (
            last[plane, own_y, :] + last[plane + 1, own_y, :]
        ) + (last[plane + 2, own_y, :] + last[plane + 3, own_y, :])
    depth = TILE // 2
    tiles = span_z // TILE
    z_id = lax.broadcasted_iota(jnp.int32, (span_z, depth * tiles), 0) // 2
    c_id = lax.broadcasted_iota(jnp.int32, (span_z, depth * tiles), 1)
    fold_z = (z_id == (c_id % tiles) * depth + c_id // tiles).astype(jnp.float32)

    def fold_y(stacked, group):
        size = stacked.shape[0]
        out_id = lax.broadcasted_iota(jnp.int32, (size // group, size), 0)
        in_id = lax.broadcasted_iota(jnp.int32, (size // group, size), 1)
        matrix = (out_id == in_id // group).astype(jnp.float32)
        part = jnp.dot(stacked, fold_z, precision=EXACT, preferred_element_type=jnp.float32)
        return jnp.dot(matrix, part, precision=EXACT, preferred_element_type=jnp.float32)

    fine = fold_y(pairs[...], 2) * 0.125
    rough = fold_y(quads[...], 4) * 0.03125
    fine_rows, rough_rows = fine.shape[0], rough.shape[0]
    for k in range(depth):
        cut = slice(tiles * k, tiles * (k + 1))
        rows_t[fine_rows * k : fine_rows * (k + 1), :] = fine[:, cut]
        start = fine_rows * depth + rough_rows * k
        rows_t[start : start + rough_rows, :] = rough[:, cut]
    send_ref[...] = lax.dot_general(
        pick_ref[...],
        rows_t[...].astype(jnp.bfloat16),
        (((1,), (1,)), ((), ())),
        preferred_element_type=jnp.float32,
    ).astype(jnp.bfloat16)


def run_slab(field, material, table, pick):
    span_x, span_y, span_z = field.shape
    width = STEPS
    block = jnp.stack([field, material.astype(jnp.float32)])
    side, low, high = halos(block, width)
    place = jnp.stack([lax.axis_index(SPACE), lax.axis_index("grp")]).astype(jnp.int32)
    planes, rows = span_x + 2 * width, span_y + 2 * PAD
    tiles = span_z // TILE
    values = (span_x * span_y // 4 + span_x * span_y // 16) * TILE // 2
    extended = pltpu.VMEM((planes, rows, span_z), jnp.float32)
    return pl.pallas_call(
        functools.partial(
            slab_kernel,
            total_x=lax.axis_size(SPACE) * span_x,
            total_y=lax.axis_size("grp") * span_y,
        ),
        out_shape=(
            jax.ShapeDtypeStruct(field.shape, jnp.float32),
            jax.ShapeDtypeStruct((pick.shape[0], values), jnp.bfloat16),
        ),
        in_specs=[SMEM, SMEM] + [VMEM] * 6,
        out_specs=(VMEM, VMEM),
        scratch_shapes=[
            extended,
            extended,
            extended,
            pltpu.VMEM((7, planes, rows, span_z), jnp.float32),
            pltpu.VMEM((span_x * span_y // 2, span_z), jnp.float32),
            pltpu.VMEM((span_x * span_y // 4, span_z), jnp.float32),
            pltpu.VMEM((values, tiles), jnp.float32),
        ],
        compiler_params=pltpu.CompilerParams(vmem_limit_bytes=LIMIT),
        name="slab",
    )(place, table, field, material, side, low, high, pick)


def slots(owner_list, tile_list, tile_count):
    shard_count, slot_count = owner_list.shape
    capacity = 2 * slot_count // shard_count
    my_index = lax.axis_index(SPACE)
    same_owner = owner_list[:, :, None] == owner_list[:, None, :]
    slot_order = jnp.arange(slot_count, dtype=jnp.int32)
    earlier = slot_order[None, :] < slot_order[:, None]
    slot_rank = jnp.sum((same_owner & earlier[None]).astype(jnp.int32), axis=2)
    owned_here = owner_list == my_index
    slot_ids = jnp.arange(capacity, dtype=jnp.int32)
    slot_match = owned_here[:, None, :] & (slot_rank[:, None, :] == slot_ids[None, :, None])
    chosen = jnp.sum(jnp.where(slot_match, tile_list[:, None, :] + 1, 0), axis=2) - 1
    tile_ids = jnp.arange(tile_count, dtype=jnp.int32)
    pick = (chosen.reshape(-1, 1) == tile_ids[None, :]).astype(jnp.bfloat16)
    own_owner = jnp.take(owner_list, my_index, axis=0)
    own_rank = jnp.take(slot_rank, my_index, axis=0)
    flat_index = own_owner * capacity + own_rank
    flat_ids = jnp.arange(shard_count * capacity, dtype=jnp.int32)
    place = (flat_index[:, None] == flat_ids[None, :]).astype(jnp.bfloat16)
    return pick, place


def forward_kernel(
    token_ref, embed_ref, gain_ref, proj_w_ref, mix_ref, read_ref,
    normed_ref, proj_ref, prob_ref, pred_ref, *base_ref,
):
    embedded = jnp.dot(
        token_ref[...], embed_ref[...], preferred_element_type=jnp.float32
    ).astype(jnp.bfloat16)
    wide = embedded.astype(jnp.float32)
    mean = jnp.mean(wide, axis=1, keepdims=True)
    removed = wide - mean
    variance = jnp.mean(removed * removed, axis=1, keepdims=True)
    normed = (removed * lax.rsqrt(variance + NORM_EPSILON) * gain_ref[...]).astype(jnp.bfloat16)
    normed_ref[...] = normed
    proj = jnp.dot(normed, proj_w_ref[...], preferred_element_type=jnp.float32).astype(jnp.bfloat16)
    proj_ref[...] = proj
    attended = []
    for seq in range(token_ref.shape[0] // SPD):
        rows = slice(seq * SPD, (seq + 1) * SPD)
        query, key, value = (proj[rows, i * HD : (i + 1) * HD] for i in range(3))
        scores = lax.dot_general(
            query, key, (((1,), (1,)), ((), ())), preferred_element_type=jnp.float32
        ) * (1.0 / math.sqrt(HD))
        raised = jnp.exp(scores - jnp.max(scores, axis=-1, keepdims=True))
        probs = raised / jnp.sum(raised, axis=-1, keepdims=True)
        prob_ref[rows, :] = probs
        attended.append(
            jnp.dot(
                probs.astype(jnp.bfloat16), value, preferred_element_type=jnp.float32
            ).astype(jnp.bfloat16)
        )
    attended = jnp.concatenate(attended, axis=0)
    pred_ref[...] = jnp.dot(
        jnp.concatenate([attended, attended], axis=1),
        mix_ref[...],
        preferred_element_type=jnp.float32,
    ).astype(pred_ref.dtype)
    if base_ref:
        base_ref[0][...] = jnp.dot(embedded, read_ref[...], preferred_element_type=jnp.float32)


def whole(array):
    return pl.BlockSpec(array.shape, lambda i: (0,) * array.ndim)


def by_rows(columns):
    return pl.BlockSpec((BLOCK_ROWS, columns), lambda i: (i, 0))


def run_forward(tokens, embed, gain, proj_w, mix, read, own):
    rows, token_width = tokens.shape
    model, heads = proj_w.shape
    out_width = read.shape[1]
    shapes = [
        jax.ShapeDtypeStruct((rows, model), jnp.bfloat16),
        jax.ShapeDtypeStruct((rows, heads), jnp.bfloat16),
        jax.ShapeDtypeStruct((rows, SPD), jnp.float32),
        jax.ShapeDtypeStruct((rows, out_width), jnp.float32 if own else jnp.bfloat16),
    ]
    if own:
        shapes.append(jax.ShapeDtypeStruct((rows, out_width), jnp.float32))
    flops = 2 * rows * model * (token_width + heads)
    return pl.pallas_call(
        forward_kernel,
        grid=(rows // BLOCK_ROWS,),
        out_shape=tuple(shapes),
        in_specs=[by_rows(token_width)]
        + [whole(array) for array in (embed, gain, proj_w, mix, read)],
        out_specs=tuple(by_rows(shape.shape[1]) for shape in shapes),
        compiler_params=pltpu.CompilerParams(vmem_limit_bytes=LIMIT),
        cost_estimate=pl.CostEstimate(
            flops=flops, bytes_accessed=rows * model * 8, transcendentals=rows * SPD
        ),
        name="forward_own" if own else "forward_other",
    )(tokens, embed, gain, proj_w, mix, read)


def backward_kernel(delta_ref, mix_t_ref, proj_ref, prob_ref, normed_ref, *rest):
    start_ref = rest[0] if len(rest) == 3 else None
    out_ref, total = rest[-2], rest[-1]
    step = pl.program_id(0)
    delta = delta_ref[...]
    grad_attended = jnp.dot(
        jnp.concatenate([delta, delta], axis=1),
        mix_t_ref[...],
        preferred_element_type=jnp.float32,
    ).astype(jnp.bfloat16)
    across = (((1,), (1,)), ((), ()))
    down = (((0,), (0,)), ((), ()))
    grads = []
    for seq in range(delta_ref.shape[0] // SPD):
        rows = slice(seq * SPD, (seq + 1) * SPD)
        query, key, value = (proj_ref[rows, i * HD : (i + 1) * HD] for i in range(3))
        upper = grad_attended[rows]
        probs = prob_ref[rows, :]
        grad_probs = lax.dot_general(upper, value, across, preferred_element_type=jnp.float32)
        grad_value = lax.dot_general(
            probs.astype(jnp.bfloat16), upper, down, preferred_element_type=jnp.float32
        )
        inner = jnp.sum(probs * grad_probs, axis=-1, keepdims=True)
        grad_scores = (probs * (grad_probs - inner) * (1.0 / math.sqrt(HD))).astype(jnp.bfloat16)
        grad_query = jnp.dot(grad_scores, key, preferred_element_type=jnp.float32)
        grad_key = lax.dot_general(grad_scores, query, down, preferred_element_type=jnp.float32)
        grads.append(
            jnp.concatenate([grad_query, grad_key, grad_value], axis=1).astype(jnp.bfloat16)
        )
    grads = jnp.concatenate(grads, axis=0)

    @pl.when(step == 0)
    def _():
        if start_ref is None:
            total[...] = jnp.zeros_like(total)
        else:
            total[...] = start_ref[...]

    total[...] += lax.dot_general(
        normed_ref[...], grads, down, preferred_element_type=jnp.float32
    )

    @pl.when(step == pl.num_programs(0) - 1)
    def _():
        if start_ref is None:
            out_ref[...] = total[...]
        else:
            for i in range(out_ref.shape[0]):
                out_ref[i] = total[:, i * HD : (i + 1) * HD].astype(out_ref.dtype)


def run_backward(delta, mix_t, proj, prob, normed, start):
    rows, model = normed.shape
    heads = proj.shape[1]
    if start is None:
        out = jax.ShapeDtypeStruct((model, heads), jnp.float32)
    else:
        out = jax.ShapeDtypeStruct((heads // HD, model, HD), jnp.bfloat16)
    operands = [delta, mix_t, proj, prob, normed]
    specs = [
        by_rows(delta.shape[1]), whole(mix_t), by_rows(heads), by_rows(SPD), by_rows(model),
    ]
    if start is not None:
        operands.append(start)
        specs.append(whole(start))
    return pl.pallas_call(
        backward_kernel,
        grid=(rows // BLOCK_ROWS,),
        out_shape=out,
        in_specs=specs,
        out_specs=whole(out),
        scratch_shapes=[pltpu.VMEM((model, heads), jnp.float32)],
        compiler_params=pltpu.CompilerParams(vmem_limit_bytes=LIMIT),
        cost_estimate=pl.CostEstimate(
            flops=2 * rows * model * heads, bytes_accessed=rows * model * 4, transcendentals=0
        ),
        name="backward_own" if start is None else "backward_other",
    )(*operands)


def sum_over_space(parts):
    count_x, count_z = lax.axis_size("x"), lax.axis_size("z")
    shape, columns = parts.shape, parts.shape[-1]
    parts = parts.reshape(count_x, -1, columns)
    part = jnp.sum(swap(parts, "x").astype(jnp.float32), axis=0)
    parts = part.astype(jnp.bfloat16).reshape(count_z, -1, columns)
    total = jnp.sum(swap(parts, "z").astype(jnp.float32), axis=0).astype(jnp.bfloat16)
    gathered = spread(total, "z").reshape(-1, columns)
    return spread(gathered, "x").reshape(shape)


def shards(
    start_field,
    material,
    conductivity,
    owners,
    tile_ids,
    embed_weight,
    layer_norm_gain,
    w_qkv,
    w_out,
    w_read,
):
    field = start_field[0]
    span_x, span_y, span_z = field.shape
    depth = TILE // 2
    token_width = embed_weight.shape[0]
    target_width = w_read.shape[1]

    embed_own = embed_weight.reshape(-1, depth, embed_weight.shape[1])
    embed_own = embed_own.transpose(1, 0, 2).reshape(embed_weight.shape)
    embed = lax.all_gather(embed_own, GROUP, axis=1, tiled=True)
    read = w_read.reshape(w_read.shape[0], -1, depth).transpose(0, 2, 1).reshape(w_read.shape)
    mixing = jnp.dot(w_out, read, preferred_element_type=jnp.float32)
    mixing_high = mixing.astype(jnp.bfloat16)
    mixing_low = (mixing - mixing_high.astype(jnp.float32)).astype(jnp.bfloat16)
    mix = jnp.concatenate([mixing_high, mixing_low], axis=0)
    mix_t = jnp.concatenate([mixing_high.T, mixing_low.T], axis=0)
    proj_w = w_qkv.transpose(1, 0, 2).reshape(w_qkv.shape[1], -1)
    gain_row = layer_norm_gain[None, :]

    pick, place = slots(owners[0, 0, :, :, 0], tile_ids[0, 0], span_z // TILE)
    final_local, send = run_slab(field, material, conductivity[0], pick)
    got = swap(send, SPACE)
    chips = lax.axis_size(CHIPS)
    copies = jnp.dot(
        jnp.tile(place, (chips, 1)), got, preferred_element_type=jnp.float32
    ).astype(jnp.bfloat16)
    samples = swap(copies, CHIPS)
    tokens, targets = samples[:, :token_width], samples[:, token_width:]

    tokens_other = swap_cores(tokens)
    weights = (embed, gain_row, proj_w, mix, read)
    normed, proj, prob, pred, base = run_forward(tokens, *weights, own=True)
    normed_other, proj_other, prob_other, pred_other = run_forward(
        tokens_other, *weights, own=False
    )
    chip_pred = (pred + swap_cores(pred_other).astype(jnp.float32)).astype(jnp.bfloat16)
    shares = spread(chip_pred, CHIPS).astype(jnp.float32)
    row_count = lax.axis_size(GROUP) * SPD
    loss_scale = math.sqrt(w_read.shape[0] / (lax.axis_size(SPACE) * row_count * target_width))
    prediction = jnp.sum(shares, axis=0) + base
    delta = ((prediction - targets.astype(jnp.float32)) * loss_scale).astype(jnp.bfloat16)

    delta_other = swap_cores(delta)
    half = run_backward(delta, mix_t, proj, prob, normed, None)
    grads = run_backward(delta_other, mix_t, proj_other, prob_other, normed_other, half)

    weight_total = sum_over_space(grads)
    gain_share = (
        jnp.sum(w_qkv.astype(jnp.float32) * weight_total.astype(jnp.float32), axis=(0, 2))
        / layer_norm_gain
    )
    gain_total = jnp.sum(spread(gain_share, GROUP), axis=0)
    return (final_local[None], weight_total, gain_total)


def solution(mesh):
    halves, space, members = (mesh.shape[name] for name in ("grp", "space", "mem"))
    fine = Mesh(
        mesh.devices.reshape(halves, space // 4, 4, members // 2, 2),
        ("grp", "z", "x", "yhi", "core"),
    )
    placed = (
        P(MEM, SPACE, "grp", None),
        P(SPACE, "grp", None),
        P(MEM, None),
        P(MEM, "grp", None, None, None),
        P(MEM, "grp", None, None),
        P(None, GROUP),
        P(),
        P(None, None, GROUP),
        P(GROUP, None),
        P(),
    )
    return jax.shard_map(
        shards,
        mesh=fine,
        in_specs=placed,
        out_specs=(P(MEM, SPACE, "grp", None), P(None, None, GROUP), P()),
        check_vma=False,
    )
```

```python
import functools
import math

import jax
import jax.numpy as jnp
from jax import lax
from jax.experimental import pallas as pl
from jax.experimental.pallas import tpu as pltpu
from jax.sharding import Mesh
from jax.sharding import PartitionSpec as P

SPD = 128
STEPS = 3
TILE = 16
HD = 128
NORM_EPSILON = 1e-06

SPACE = ("z", "x")
MEM = ("yhi", "core")
GROUP = ("grp", "yhi", "core")
CHIPS = ("grp", "yhi")

PAD = 4
BLOCK_ROWS = 256
VMEM = pl.BlockSpec(memory_space=pltpu.VMEM)
SMEM = pl.BlockSpec(memory_space=pltpu.SMEM)
LIMIT = 20 * 1024 * 1024
EXACT = lax.Precision.HIGHEST


def swap(parts, axis):
    return lax.all_to_all(parts, axis, split_axis=0, concat_axis=0, tiled=True)


def spread(own, axis):
    count = lax.axis_size(axis)
    return swap(jnp.broadcast_to(own[None], (count,) + own.shape), axis)


def swap_with(own, axis):
    return lax.ppermute(own, axis, [(0, 1), (1, 0)])


def swap_cores(own):
    return swap_with(own, "core")


def halos(block, width, beside):
    half = lax.axis_index("grp")
    face = jnp.where(half == 0, block[:, :, -width:], block[:, :, :width])
    side = swap_with(face, "grp")
    side, beside = lax.optimization_barrier((side, beside))
    count = lax.axis_size(SPACE)
    forward = [(i, i + 1) for i in range(count - 1)]
    backward = [(i + 1, i) for i in range(count - 1)]
    top = jnp.concatenate([side[:, -width:], block[:, -width:], side[:, -width:]], axis=2)
    bottom = jnp.concatenate([side[:, :width], block[:, :width], side[:, :width]], axis=2)
    low = lax.ppermute(top, SPACE, forward)
    high = lax.ppermute(bottom, SPACE, backward)
    return side, low, high, beside


def over(first, last, body):
    def turn(i, _):
        body(first + 2 * i)
        body(first + 2 * i + 1)
        return 0

    lax.fori_loop(0, (last - first) // 2, turn, 0)
    if (last - first) % 2:
        body(last - 1)


def slab_kernel(
    place_ref,
    table_ref,
    field_ref,
    material_ref,
    side_ref,
    low_ref,
    high_ref,
    pick_ref,
    final_ref,
    send_ref,
    field_a,
    field_b,
    cond,
    coef,
    pairs,
    quads,
    rows_t,
    *,
    total_x,
    total_y,
):
    span_x, span_y, span_z = field_ref.shape
    width = low_ref.shape[1]
    rows = span_y + 2 * PAD
    planes = span_x + 2 * width
    own_x = slice(width, width + span_x)
    own_y = slice(PAD, PAD + span_y)
    ext_y = slice(PAD - width, PAD + span_y + width)

    field_a[...] = jnp.zeros_like(field_a)
    cond[...] = jnp.zeros_like(cond)
    for part, target in ((0, field_a), (1, cond)):
        target[own_x, slice(PAD - width, PAD), :] = side_ref[part]
        target[own_x, slice(PAD + span_y, PAD + span_y + width), :] = side_ref[part]
        target[slice(0, width), ext_y, :] = low_ref[part]
        target[slice(width + span_x, planes), ext_y, :] = high_ref[part]
    field_a[own_x, own_y, :] = field_ref[...]
    cond[own_x, own_y, :] = material_ref[...].astype(jnp.float32)

    place_x = place_ref[0] * span_x - width
    place_y = place_ref[1] * span_y - PAD
    row_id = place_y + lax.broadcasted_iota(jnp.int32, (rows, span_z), 0)
    col_id = lax.broadcasted_iota(jnp.int32, (rows, span_z), 1)
    inside_y = (row_id >= 0) & (row_id < total_y)
    first_z = col_id == 0
    last_z = col_id == span_z - 1

    def inside(plane):
        at = place_x + plane
        in_x = ((at >= 0) & (at < total_x)).astype(jnp.int32)
        return inside_y & (jnp.full((rows, span_z), in_x) > 0)

    def set_cond(plane):
        kind = cond[plane]
        value = jnp.zeros_like(kind)
        for level in range(table_ref.shape[0]):
            value = jnp.where(kind == float(level), table_ref[level], value)
        keep = inside(plane)
        cond[plane] = jnp.where(keep, value, 0.0)
        field_a[plane] = jnp.where(keep, field_a[plane], 0.0)

    over(0, planes, set_cond)

    def set_coef(plane):
        mine = 0.5 * cond[plane]
        keep = inside(plane)
        ups = mine + pltpu.roll(mine, 1, 0)
        downs = mine + pltpu.roll(mine, rows - 1, 0)
        before = mine + jnp.where(first_z, 0.0, pltpu.roll(mine, 1, 1))
        after = mine + jnp.where(last_z, 0.0, pltpu.roll(mine, span_z - 1, 1))
        left = mine + 0.5 * cond[plane - 1]
        right = mine + 0.5 * cond[plane + 1]
        rest = 1.0 - (ups + downs + before + after + left + right)
        coef[0, plane] = jnp.where(keep, rest, 0.0)
        coef[1, plane] = jnp.where(keep, left, 0.0)
        coef[2, plane] = jnp.where(keep, right, 0.0)
        coef[3, plane] = jnp.where(keep, ups, 0.0)
        coef[4, plane] = jnp.where(keep, downs, 0.0)
        coef[5, plane] = jnp.where(keep & ~first_z, before, 0.0)
        coef[6, plane] = jnp.where(keep & ~last_z, after, 0.0)

    over(1, planes - 1, set_coef)

    def step(source, target):
        def one(plane):
            mid = source[plane]
            value = coef[0, plane] * mid
            value = value + coef[1, plane] * source[plane - 1]
            value = value + coef[2, plane] * source[plane + 1]
            value = value + coef[3, plane] * pltpu.roll(mid, 1, 0)
            value = value + coef[4, plane] * pltpu.roll(mid, rows - 1, 0)
            value = value + coef[5, plane] * pltpu.roll(mid, 1, 1)
            value = value + coef[6, plane] * pltpu.roll(mid, span_z - 1, 1)
            target[plane] = value

        return one

    for number in range(STEPS):
        source, target = (field_a, field_b) if number % 2 == 0 else (field_b, field_a)
        over(1 + number, planes - 1 - number, step(source, target))

    before_last, last = (field_a, field_b) if STEPS % 2 == 1 else (field_b, field_a)
    final_ref[...] = last[own_x, own_y, :]

    for i in range(span_x // 2):
        plane = width + 2 * i
        pairs[span_y * i : span_y * (i + 1), :] = (
            before_last[plane, own_y, :] + before_last[plane + 1, own_y, :]
        )
    for i in range(span_x // 4):
        plane = width + 4 * i
        quads[span_y * i : span_y * (i + 1), :] = (
            last[plane, own_y, :] + last[plane + 1, own_y, :]
        ) + (last[plane + 2, own_y, :] + last[plane + 3, own_y, :])
    depth = TILE // 2
    tiles = span_z // TILE
    z_id = lax.broadcasted_iota(jnp.int32, (span_z, depth * tiles), 0) // 2
    c_id = lax.broadcasted_iota(jnp.int32, (span_z, depth * tiles), 1)
    fold_z = (z_id == (c_id % tiles) * depth + c_id // tiles).astype(jnp.float32)

    def fold_y(stacked, group):
        size = stacked.shape[0]
        out_id = lax.broadcasted_iota(jnp.int32, (size // group, size), 0)
        in_id = lax.broadcasted_iota(jnp.int32, (size // group, size), 1)
        matrix = (out_id == in_id // group).astype(jnp.float32)
        part = jnp.dot(stacked, fold_z, precision=EXACT, preferred_element_type=jnp.float32)
        return jnp.dot(matrix, part, precision=EXACT, preferred_element_type=jnp.float32)

    fine = fold_y(pairs[...], 2) * 0.125
    rough = fold_y(quads[...], 4) * 0.03125
    fine_rows, rough_rows = fine.shape[0], rough.shape[0]
    for k in range(depth):
        cut = slice(tiles * k, tiles * (k + 1))
        rows_t[pl.ds(k, fine_rows, stride=depth), :] = fine[:, cut]
        rows_t[pl.ds(fine_rows * depth + k, rough_rows, stride=depth), :] = rough[:, cut]
    send_ref[...] = lax.dot_general(
        pick_ref[...],
        rows_t[...].astype(jnp.bfloat16),
        (((1,), (1,)), ((), ())),
        preferred_element_type=jnp.float32,
    ).astype(jnp.bfloat16)


def run_slab(field, material, table, owner_list, tile_list, embed_own):
    span_x, span_y, span_z = field.shape
    width = STEPS
    block = jnp.stack([field, material.astype(jnp.float32)])
    side, low, high, (owner_list, embed_own) = halos(block, width, (owner_list, embed_own))
    embed = jnp.stack([embed_own, swap_with(embed_own, "yhi")])
    pick, place = slots(owner_list, tile_list, span_z // TILE)
    origin = jnp.stack([lax.axis_index(SPACE), lax.axis_index("grp")]).astype(jnp.int32)
    planes, rows = span_x + 2 * width, span_y + 2 * PAD
    tiles = span_z // TILE
    values = (span_x * span_y // 4 + span_x * span_y // 16) * TILE // 2
    extended = pltpu.VMEM((planes, rows, span_z), jnp.float32)
    final, send = pl.pallas_call(
        functools.partial(
            slab_kernel,
            total_x=lax.axis_size(SPACE) * span_x,
            total_y=lax.axis_size("grp") * span_y,
        ),
        out_shape=(
            jax.ShapeDtypeStruct(field.shape, jnp.float32),
            jax.ShapeDtypeStruct((pick.shape[0], values), jnp.bfloat16),
        ),
        in_specs=[SMEM, SMEM] + [VMEM] * 6,
        out_specs=(VMEM, VMEM),
        scratch_shapes=[
            extended,
            extended,
            extended,
            pltpu.VMEM((7, planes, rows, span_z), jnp.float32),
            pltpu.VMEM((span_x * span_y // 2, span_z), jnp.float32),
            pltpu.VMEM((span_x * span_y // 4, span_z), jnp.float32),
            pltpu.VMEM((values, tiles), jnp.float32),
        ],
        compiler_params=pltpu.CompilerParams(vmem_limit_bytes=LIMIT),
        name="slab",
    )(origin, table, field, material, side, low, high, pick)
    return final, send, place, embed


def slots(owner_list, tile_list, tile_count):
    shard_count, slot_count = owner_list.shape
    capacity = 2 * slot_count // shard_count
    my_index = lax.axis_index(SPACE)
    same_owner = owner_list[:, :, None] == owner_list[:, None, :]
    slot_order = jnp.arange(slot_count, dtype=jnp.int32)
    earlier = slot_order[None, :] < slot_order[:, None]
    slot_rank = jnp.sum((same_owner & earlier[None]).astype(jnp.int32), axis=2)
    owned_here = owner_list == my_index
    slot_ids = jnp.arange(capacity, dtype=jnp.int32)
    slot_match = owned_here[:, None, :] & (slot_rank[:, None, :] == slot_ids[None, :, None])
    chosen = jnp.sum(jnp.where(slot_match, tile_list[:, None, :] + 1, 0), axis=2) - 1
    tile_ids = jnp.arange(tile_count, dtype=jnp.int32)
    pick = (chosen.reshape(-1, 1) == tile_ids[None, :]).astype(jnp.bfloat16)
    own_owner = jnp.take(owner_list, my_index, axis=0)
    own_rank = jnp.take(slot_rank, my_index, axis=0)
    flat_index = own_owner * capacity + own_rank
    flat_ids = jnp.arange(shard_count * capacity, dtype=jnp.int32)
    place = (flat_index[:, None] == flat_ids[None, :]).astype(jnp.bfloat16)
    return pick, place


def mixing_parts(out_ref, read_ref):
    mixing = jnp.dot(out_ref[...], read_ref[...], preferred_element_type=jnp.float32)
    high = mixing.astype(jnp.bfloat16)
    return high, (mixing - high.astype(jnp.float32)).astype(jnp.bfloat16)


def forward_kernel(
    sample_ref, embed_ref, gain_ref, proj_w_ref, out_ref, read_ref,
    normed_ref, proj_ref, prob_ref, pred_ref, *base_ref,
):
    embedded = jnp.dot(
        sample_ref[:, : embed_ref.shape[0]], embed_ref[...], preferred_element_type=jnp.float32
    ).astype(jnp.bfloat16)
    wide = embedded.astype(jnp.float32)
    mean = jnp.mean(wide, axis=1, keepdims=True)
    removed = wide - mean
    variance = jnp.mean(removed * removed, axis=1, keepdims=True)
    normed = (removed * lax.rsqrt(variance + NORM_EPSILON) * gain_ref[...]).astype(jnp.bfloat16)
    normed_ref[...] = normed
    proj_w = jnp.concatenate([proj_w_ref[i] for i in range(3)], axis=1)
    proj = jnp.dot(normed, proj_w, preferred_element_type=jnp.float32).astype(jnp.bfloat16)
    proj_ref[...] = proj
    attended = []
    for seq in range(sample_ref.shape[0] // SPD):
        rows = slice(seq * SPD, (seq + 1) * SPD)
        query, key, value = (proj[rows, i * HD : (i + 1) * HD] for i in range(3))
        scores = lax.dot_general(
            query, key, (((1,), (1,)), ((), ())), preferred_element_type=jnp.float32
        ) * (1.0 / math.sqrt(HD))
        raised = jnp.exp(scores - jnp.max(scores, axis=-1, keepdims=True))
        probs = raised / jnp.sum(raised, axis=-1, keepdims=True)
        prob_ref[rows, :] = probs
        attended.append(
            jnp.dot(
                probs.astype(jnp.bfloat16), value, preferred_element_type=jnp.float32
            ).astype(jnp.bfloat16)
        )
    attended = jnp.concatenate(attended, axis=0)
    high, low = mixing_parts(out_ref, read_ref)
    pred_ref[...] = jnp.dot(
        jnp.concatenate([attended, attended], axis=1),
        jnp.concatenate([high, low], axis=0),
        preferred_element_type=jnp.float32,
    ).astype(pred_ref.dtype)
    if base_ref:
        targets = sample_ref[:, embed_ref.shape[0] :].astype(jnp.float32)
        base_ref[0][...] = (
            jnp.dot(embedded, read_ref[...], preferred_element_type=jnp.float32) - targets
        )


def whole(array):
    return pl.BlockSpec(
        array.shape, lambda i: (0,) * array.ndim, pipeline_mode=pl.Buffered(buffer_count=1)
    )


def by_rows(columns):
    return pl.BlockSpec((BLOCK_ROWS, columns), lambda i: (i, 0))


def run_forward(samples, embed, gain, w_qkv, w_out, w_read, own):
    rows, sample_width = samples.shape
    kinds, model, head = w_qkv.shape
    out_width = w_read.shape[1]
    shapes = [
        jax.ShapeDtypeStruct((rows, model), jnp.bfloat16),
        jax.ShapeDtypeStruct((rows, kinds * head), jnp.bfloat16),
        jax.ShapeDtypeStruct((rows, SPD), jnp.float32),
        jax.ShapeDtypeStruct((rows, out_width), jnp.float32 if own else jnp.bfloat16),
    ]
    if own:
        shapes.append(jax.ShapeDtypeStruct((rows, out_width), jnp.float32))
    weights = (embed, gain, w_qkv, w_out, w_read)
    return pl.pallas_call(
        forward_kernel,
        grid=(rows // BLOCK_ROWS,),
        out_shape=tuple(shapes),
        in_specs=[by_rows(sample_width)] + [whole(array) for array in weights],
        out_specs=tuple(by_rows(shape.shape[1]) for shape in shapes),
        compiler_params=pltpu.CompilerParams(vmem_limit_bytes=LIMIT),
        cost_estimate=pl.CostEstimate(
            flops=2 * rows * model * (embed.shape[0] + kinds * head),
            bytes_accessed=rows * model * 8,
            transcendentals=rows * SPD,
        ),
        name="forward_own" if own else "forward_other",
    )(samples, *weights)


def delta_kernel(share_ref, base_ref, delta_ref, *, scale):
    total = base_ref[...]
    for i in range(share_ref.shape[0]):
        total = total + share_ref[i].astype(jnp.float32)
    delta_ref[...] = (total * scale).astype(delta_ref.dtype)


def run_delta(shares, base, scale):
    return pl.pallas_call(
        functools.partial(delta_kernel, scale=scale),
        out_shape=jax.ShapeDtypeStruct(base.shape, jnp.bfloat16),
        in_specs=[VMEM, VMEM],
        out_specs=VMEM,
        compiler_params=pltpu.CompilerParams(vmem_limit_bytes=LIMIT),
        name="delta",
    )(shares, base)


def backward_kernel(delta_ref, out_ref, read_ref, proj_ref, prob_ref, normed_ref, *rest):
    start_ref = rest[0] if len(rest) == 3 else None
    grad_ref, total = rest[-2], rest[-1]
    step = pl.program_id(0)
    across = (((1,), (1,)), ((), ()))
    down = (((0,), (0,)), ((), ()))
    delta = delta_ref[...]
    high, low = mixing_parts(out_ref, read_ref)
    grad_attended = lax.dot_general(
        jnp.concatenate([delta, delta], axis=1),
        jnp.concatenate([high, low], axis=1),
        across,
        preferred_element_type=jnp.float32,
    ).astype(jnp.bfloat16)
    grads = []
    for seq in range(delta_ref.shape[0] // SPD):
        rows = slice(seq * SPD, (seq + 1) * SPD)
        query, key, value = (proj_ref[rows, i * HD : (i + 1) * HD] for i in range(3))
        upper = grad_attended[rows]
        probs = prob_ref[rows, :]
        grad_probs = lax.dot_general(upper, value, across, preferred_element_type=jnp.float32)
        grad_value = lax.dot_general(
            probs.astype(jnp.bfloat16), upper, down, preferred_element_type=jnp.float32
        )
        inner = jnp.sum(probs * grad_probs, axis=-1, keepdims=True)
        grad_scores = (probs * (grad_probs - inner) * (1.0 / math.sqrt(HD))).astype(jnp.bfloat16)
        grad_query = jnp.dot(grad_scores, key, preferred_element_type=jnp.float32)
        grad_key = lax.dot_general(grad_scores, query, down, preferred_element_type=jnp.float32)
        grads.append(
            jnp.concatenate([grad_query, grad_key, grad_value], axis=1).astype(jnp.bfloat16)
        )
    grads = jnp.concatenate(grads, axis=0)

    @pl.when(step == 0)
    def _():
        if start_ref is None:
            total[...] = jnp.zeros_like(total)
        else:
            total[...] = start_ref[...]

    total[...] += lax.dot_general(
        normed_ref[...], grads, down, preferred_element_type=jnp.float32
    )

    @pl.when(step == pl.num_programs(0) - 1)
    def _():
        if start_ref is None:
            grad_ref[...] = total[...]
        else:
            for i in range(grad_ref.shape[0]):
                grad_ref[i] = total[:, i * HD : (i + 1) * HD].astype(grad_ref.dtype)


def run_backward(delta, w_out, w_read, proj, prob, normed, start):
    rows, model = normed.shape
    heads = proj.shape[1]
    if start is None:
        out = jax.ShapeDtypeStruct((model, heads), jnp.float32)
    else:
        out = jax.ShapeDtypeStruct((heads // HD, model, HD), jnp.bfloat16)
    operands = [delta, w_out, w_read, proj, prob, normed]
    specs = [
        by_rows(delta.shape[1]), whole(w_out), whole(w_read),
        by_rows(heads), by_rows(SPD), by_rows(model),
    ]
    if start is not None:
        operands.append(start)
        specs.append(whole(start))
    return pl.pallas_call(
        backward_kernel,
        grid=(rows // BLOCK_ROWS,),
        out_shape=out,
        in_specs=specs,
        out_specs=whole(out),
        scratch_shapes=[pltpu.VMEM((model, heads), jnp.float32)],
        compiler_params=pltpu.CompilerParams(vmem_limit_bytes=LIMIT),
        cost_estimate=pl.CostEstimate(
            flops=2 * rows * model * heads, bytes_accessed=rows * model * 4, transcendentals=0
        ),
        name="backward_own" if start is None else "backward_other",
    )(*operands)


def split(values, rows):
    columns = 128
    high = values.astype(jnp.bfloat16)
    low = (values - high.astype(jnp.float32)).astype(jnp.bfloat16)
    both = jnp.stack([high, low], axis=-2)
    both = both.reshape(both.shape[:-2] + (-1, min(columns, both.shape[-1])))
    pad = [(0, 0)] * (both.ndim - 2)
    return jnp.pad(both, pad + [(0, rows - both.shape[-2]), (0, columns - both.shape[-1])])


def sum_over_devices(parts, gain):
    count_x, count_z = lax.axis_size("x"), lax.axis_size("z")
    shape, columns, width = parts.shape, parts.shape[-1], gain.shape[0]
    chunk = width // count_z
    spare = 8

    part = jnp.sum(swap(parts.reshape(count_x, -1, columns), "x").astype(jnp.float32), axis=0)
    for axis in ("core", "grp", "yhi"):
        gain = gain + swap_with(gain, axis)

    sent = jnp.concatenate(
        [
            part.astype(jnp.bfloat16).reshape(count_z, -1, columns),
            split(gain.reshape(count_z, chunk), spare),
        ],
        axis=1,
    )
    total = jnp.sum(swap(sent, "z").astype(jnp.float32), axis=0)
    rows = total.shape[0] - spare
    own_gain = total[rows, :chunk] + total[rows + 1, :chunk]
    sent = jnp.concatenate([total[:rows].astype(jnp.bfloat16), split(own_gain, spare)], axis=0)
    got = spread(sent, "z").reshape(count_z, -1, columns)
    gain = (
        got[:, rows, :chunk].astype(jnp.float32) + got[:, rows + 1, :chunk].astype(jnp.float32)
    ).reshape(width)
    gain_rows = 2 * width // columns
    sent = jnp.concatenate([got[:, :rows].reshape(-1, columns), split(gain, gain_rows)], axis=0)
    got = spread(sent, "x").reshape(count_x, -1, columns)
    gain = jnp.sum(got[:, -gain_rows:].astype(jnp.float32), axis=0)
    gain = (gain[: gain_rows // 2] + gain[gain_rows // 2 :]).reshape(width)
    return got[:, :-gain_rows].reshape(shape), gain


def shards(
    start_field,
    material,
    conductivity,
    owners,
    tile_ids,
    embed_weight,
    layer_norm_gain,
    w_qkv,
    w_out,
    w_read,
):
    gain_row = layer_norm_gain[None, :]
    final_local, send, place, embed = run_slab(
        start_field[0],
        material,
        conductivity[0],
        owners[0, 0, :, :, 0],
        tile_ids[0, 0],
        embed_weight,
    )
    send, embed = lax.optimization_barrier((send, embed))
    got = swap(send, SPACE)
    embed = jnp.stack([embed, swap_with(embed, "grp")])
    embed = jnp.stack([embed, swap_cores(embed)]).reshape((-1,) + embed_weight.shape)
    away = lax.axis_index(GROUP) ^ jnp.arange(embed.shape[0], dtype=jnp.int32)
    embed = embed[((away & 1) << 2) + ((away >> 2 & 1) << 1) + (away >> 1 & 1)]
    embed = embed.transpose(1, 0, 2).reshape(embed_weight.shape[0], -1)

    chips = lax.axis_size(CHIPS)
    copies = jnp.dot(
        jnp.tile(place, (chips, 1)), got, preferred_element_type=jnp.float32
    ).astype(jnp.bfloat16)
    copies, embed = lax.optimization_barrier((copies, embed))
    samples = swap(copies, CHIPS)

    samples_other = swap_cores(samples)
    weights = (embed, gain_row, w_qkv, w_out, w_read)
    normed, proj, prob, pred, base = run_forward(samples, *weights, own=True)
    normed_other, proj_other, prob_other, pred_other = run_forward(
        samples_other, *weights, own=False
    )
    chip_pred = (pred + swap_cores(pred_other).astype(jnp.float32)).astype(jnp.bfloat16)
    shares = spread(chip_pred, CHIPS).reshape((chips,) + base.shape)
    row_count = lax.axis_size(GROUP) * SPD
    loss_scale = math.sqrt(
        w_read.shape[0] / (lax.axis_size(SPACE) * row_count * w_read.shape[1])
    )
    delta = run_delta(shares, base, loss_scale)

    delta_other = swap_cores(delta)
    half = run_backward(delta, w_out, w_read, proj, prob, normed, None)
    grads = run_backward(
        delta_other, w_out, w_read, proj_other, prob_other, normed_other, half
    )

    gain_share = (
        jnp.sum(w_qkv.astype(jnp.float32) * grads.astype(jnp.float32), axis=(0, 2))
        / layer_norm_gain
    )
    weight_total, gain_total = sum_over_devices(grads, gain_share)
    return (final_local[None], weight_total, gain_total)


def solution(mesh):
    halves, space, members = (mesh.shape[name] for name in ("grp", "space", "mem"))
    fine = Mesh(
        mesh.devices.reshape(halves, space // 4, 4, members // 2, 2),
        ("grp", "z", "x", "yhi", "core"),
    )
    placed = (
        P(MEM, SPACE, "grp", None),
        P(SPACE, "grp", None),
        P(MEM, None),
        P(MEM, "grp", None, None, None),
        P(MEM, "grp", None, None),
        P(None, GROUP),
        P(),
        P(None, None, GROUP),
        P(GROUP, None),
        P(),
    )
    return jax.shard_map(
        shards,
        mesh=fine,
        in_specs=placed,
        out_specs=(P(MEM, SPACE, "grp", None), P(None, None, GROUP), P()),
        check_vma=False,
    )
```

```python
import functools
import math

import jax
import jax.numpy as jnp
from jax import lax
from jax.experimental import pallas as pl
from jax.experimental.pallas import tpu as pltpu
from jax.sharding import Mesh
from jax.sharding import PartitionSpec as P

SPD = 128
STEPS = 3
TILE = 16
HD = 128
NORM_EPSILON = 1e-06

SPACE = ("z", "x")
MEM = ("yhi", "core")
GROUP = ("grp", "yhi", "core")
CHIPS = ("grp", "yhi")

PAD = 4
VMEM = pl.BlockSpec(memory_space=pltpu.VMEM)
SMEM = pl.BlockSpec(memory_space=pltpu.SMEM)
LIMIT = 20 * 1024 * 1024
EXACT = lax.Precision.HIGHEST


def swap(parts, axis):
    return lax.all_to_all(parts, axis, split_axis=0, concat_axis=0, tiled=True)


def spread(own, axis):
    count = lax.axis_size(axis)
    return swap(jnp.broadcast_to(own[None], (count,) + own.shape), axis)


def swap_with(own, axis):
    return lax.ppermute(own, axis, [(0, 1), (1, 0)])


def swap_cores(own):
    return swap_with(own, "core")


def halos(field, material, width, beside):
    half = lax.axis_index("grp")

    def cut(span, axis):
        return jnp.stack(
            [
                lax.slice_in_dim(field, *span, axis=axis),
                lax.slice_in_dim(material, *span, axis=axis).astype(jnp.float32),
            ]
        )

    span_x, span_y = field.shape[:2]
    face = jnp.where(
        half == 0, cut((span_y - width, span_y), 1), cut((0, width), 1)
    )
    side = swap_with(face, "grp")
    side, beside = lax.optimization_barrier((side, beside))
    count = lax.axis_size(SPACE)
    forward = [(i, i + 1) for i in range(count - 1)]
    backward = [(i + 1, i) for i in range(count - 1)]
    top, bottom = side[:, -width:], side[:, :width]
    top = jnp.concatenate([top, cut((span_x - width, span_x), 0), top], axis=2)
    bottom = jnp.concatenate([bottom, cut((0, width), 0), bottom], axis=2)
    low = lax.ppermute(top, SPACE, forward)
    high = lax.ppermute(bottom, SPACE, backward)
    return side, low, high, beside


def over(first, last, body):
    for plane in range(first, last):
        body(plane)


def slab_kernel(
    place_ref,
    table_ref,
    field_ref,
    material_ref,
    side_ref,
    low_ref,
    high_ref,
    pick_ref,
    final_ref,
    send_ref,
    field_a,
    field_b,
    cond,
    coef,
    pairs,
    quads,
    rows_t,
    *,
    total_x,
    total_y,
):
    span_x, span_y, span_z = field_ref.shape
    width = low_ref.shape[1]
    rows = span_y + 2 * PAD
    planes = span_x + 2 * width
    own_x = slice(width, width + span_x)
    own_y = slice(PAD, PAD + span_y)
    ext_y = slice(PAD - width, PAD + span_y + width)

    field_a[...] = jnp.zeros_like(field_a)
    cond[...] = jnp.zeros_like(cond)
    for part, target in ((0, field_a), (1, cond)):
        target[own_x, slice(PAD - width, PAD), :] = side_ref[part]
        target[own_x, slice(PAD + span_y, PAD + span_y + width), :] = side_ref[part]
        target[slice(0, width), ext_y, :] = low_ref[part]
        target[slice(width + span_x, planes), ext_y, :] = high_ref[part]
    field_a[own_x, own_y, :] = field_ref[...]
    cond[own_x, own_y, :] = material_ref[...].astype(jnp.float32)

    place_x = place_ref[0] * span_x - width
    place_y = place_ref[1] * span_y - PAD
    row_id = place_y + lax.broadcasted_iota(jnp.int32, (rows, span_z), 0)
    col_id = lax.broadcasted_iota(jnp.int32, (rows, span_z), 1)
    inside_y = (row_id >= 0) & (row_id < total_y)
    first_z = col_id == 0
    last_z = col_id == span_z - 1

    def inside(plane):
        at = place_x + plane
        in_x = ((at >= 0) & (at < total_x)).astype(jnp.int32)
        return inside_y & (jnp.full((rows, span_z), in_x) > 0)

    def set_cond(plane):
        kind = cond[plane]
        value = jnp.zeros_like(kind)
        for level in range(table_ref.shape[0]):
            value = jnp.where(kind == float(level), table_ref[level], value)
        keep = inside(plane)
        cond[plane] = jnp.where(keep, value, 0.0)
        field_a[plane] = jnp.where(keep, field_a[plane], 0.0)

    over(0, planes, set_cond)

    def set_coef(plane):
        mine = 0.5 * cond[plane]
        keep = inside(plane)
        ups = mine + pltpu.roll(mine, 1, 0)
        downs = mine + pltpu.roll(mine, rows - 1, 0)
        before = mine + jnp.where(first_z, 0.0, pltpu.roll(mine, 1, 1))
        after = mine + jnp.where(last_z, 0.0, pltpu.roll(mine, span_z - 1, 1))
        left = mine + 0.5 * cond[plane - 1]
        right = mine + 0.5 * cond[plane + 1]
        rest = 1.0 - (ups + downs + before + after + left + right)
        coef[0, plane] = jnp.where(keep, rest, 0.0)
        coef[1, plane] = jnp.where(keep, left, 0.0)
        coef[2, plane] = jnp.where(keep, right, 0.0)
        coef[3, plane] = jnp.where(keep, ups, 0.0)
        coef[4, plane] = jnp.where(keep, downs, 0.0)
        coef[5, plane] = jnp.where(keep & ~first_z, before, 0.0)
        coef[6, plane] = jnp.where(keep & ~last_z, after, 0.0)

    over(1, planes - 1, set_coef)

    def step(source, target):
        def one(plane):
            mid = source[plane]
            value = coef[0, plane] * mid
            value = value + coef[1, plane] * source[plane - 1]
            value = value + coef[2, plane] * source[plane + 1]
            value = value + coef[3, plane] * pltpu.roll(mid, 1, 0)
            value = value + coef[4, plane] * pltpu.roll(mid, rows - 1, 0)
            value = value + coef[5, plane] * pltpu.roll(mid, 1, 1)
            value = value + coef[6, plane] * pltpu.roll(mid, span_z - 1, 1)
            target[plane] = value

        return one

    for number in range(STEPS):
        source, target = (field_a, field_b) if number % 2 == 0 else (field_b, field_a)
        over(1 + number, planes - 1 - number, step(source, target))

    before_last, last = (field_a, field_b) if STEPS % 2 == 1 else (field_b, field_a)
    final_ref[...] = last[own_x, own_y, :]

    for i in range(span_x // 2):
        plane = width + 2 * i
        pairs[span_y * i : span_y * (i + 1), :] = (
            before_last[plane, own_y, :] + before_last[plane + 1, own_y, :]
        )
    for i in range(span_x // 4):
        plane = width + 4 * i
        quads[span_y * i : span_y * (i + 1), :] = (
            last[plane, own_y, :] + last[plane + 1, own_y, :]
        ) + (last[plane + 2, own_y, :] + last[plane + 3, own_y, :])
    depth = TILE // 2
    tiles = span_z // TILE
    z_id = lax.broadcasted_iota(jnp.int32, (span_z, depth * tiles), 0) // 2
    c_id = lax.broadcasted_iota(jnp.int32, (span_z, depth * tiles), 1)
    fold_z = (z_id == (c_id % tiles) * depth + c_id // tiles).astype(jnp.float32)

    def fold_y(stacked, group):
        size = stacked.shape[0]
        out_id = lax.broadcasted_iota(jnp.int32, (size // group, size), 0)
        in_id = lax.broadcasted_iota(jnp.int32, (size // group, size), 1)
        matrix = (out_id == in_id // group).astype(jnp.float32)
        part = jnp.dot(stacked, fold_z, precision=EXACT, preferred_element_type=jnp.float32)
        return jnp.dot(matrix, part, precision=EXACT, preferred_element_type=jnp.float32)

    fine = fold_y(pairs[...], 2) * 0.125
    rough = fold_y(quads[...], 4) * 0.03125
    fine_rows, rough_rows = fine.shape[0], rough.shape[0]
    for k in range(depth):
        cut = slice(tiles * k, tiles * (k + 1))
        rows_t[pl.ds(k, fine_rows, stride=depth), :] = fine[:, cut]
        rows_t[pl.ds(fine_rows * depth + k, rough_rows, stride=depth), :] = rough[:, cut]
    send_ref[...] = lax.dot_general(
        pick_ref[...],
        rows_t[...].astype(jnp.bfloat16),
        (((1,), (1,)), ((), ())),
        preferred_element_type=jnp.float32,
    ).astype(jnp.bfloat16)


def run_slab(field, material, table, owner_list, tile_list, embed_own):
    pick, place = slots(owner_list, tile_list, field.shape[2] // TILE)
    side, low, high, embed_own = halos(field, material, STEPS, embed_own)
    embed = jnp.stack([embed_own, swap_with(embed_own, "yhi")])
    origin = jnp.stack([lax.axis_index(SPACE), lax.axis_index("grp")]).astype(jnp.int32)
    totals = (lax.axis_size(SPACE) * field.shape[0], lax.axis_size("grp") * field.shape[1])
    final, send = call_slab(origin, table, field, material, side, low, high, pick, totals)
    return final, send, place, embed


def call_slab(origin, table, field, material, side, low, high, pick, totals):
    span_x, span_y, span_z = field.shape
    planes, rows = span_x + 2 * low.shape[1], span_y + 2 * PAD
    tiles = span_z // TILE
    values = (span_x * span_y // 4 + span_x * span_y // 16) * TILE // 2
    extended = pltpu.VMEM((planes, rows, span_z), jnp.float32)
    return pl.pallas_call(
        functools.partial(slab_kernel, total_x=totals[0], total_y=totals[1]),
        out_shape=(
            jax.ShapeDtypeStruct(field.shape, jnp.float32),
            jax.ShapeDtypeStruct((pick.shape[0], values), jnp.bfloat16),
        ),
        in_specs=[SMEM, SMEM] + [VMEM] * 6,
        out_specs=(VMEM, VMEM),
        scratch_shapes=[
            extended,
            extended,
            extended,
            pltpu.VMEM((7, planes, rows, span_z), jnp.float32),
            pltpu.VMEM((span_x * span_y // 2, span_z), jnp.float32),
            pltpu.VMEM((span_x * span_y // 4, span_z), jnp.float32),
            pltpu.VMEM((values, tiles), jnp.float32),
        ],
        compiler_params=pltpu.CompilerParams(vmem_limit_bytes=LIMIT),
        name="slab",
    )(origin, table, field, material, side, low, high, pick)


def slots(owner_list, tile_list, tile_count):
    shard_count, slot_count = owner_list.shape
    capacity = 2 * slot_count // shard_count
    my_index = lax.axis_index(SPACE)
    slot_order = jnp.arange(slot_count, dtype=jnp.int32)
    earlier = slot_order[:, None] < slot_order[None, :]
    owned_here = owner_list == my_index
    here_rank = jnp.dot(
        owned_here.astype(jnp.bfloat16),
        earlier.astype(jnp.bfloat16),
        preferred_element_type=jnp.float32,
    ).astype(jnp.int32)
    slot_ids = jnp.arange(capacity, dtype=jnp.int32)
    slot_match = owned_here[:, None, :] & (here_rank[:, None, :] == slot_ids[None, :, None])
    chosen = jnp.sum(jnp.where(slot_match, tile_list[:, None, :] + 1, 0), axis=2) - 1
    tile_ids = jnp.arange(tile_count, dtype=jnp.int32)
    pick = (chosen.reshape(-1, 1) == tile_ids[None, :]).astype(jnp.bfloat16)
    own_owner = jnp.take(owner_list, my_index, axis=0)
    same_owner = own_owner[:, None] == own_owner[None, :]
    own_rank = jnp.sum((same_owner & earlier).astype(jnp.int32), axis=0)
    flat_index = own_owner * capacity + own_rank
    flat_ids = jnp.arange(shard_count * capacity, dtype=jnp.int32)
    place = (flat_index[:, None] == flat_ids[None, :]).astype(jnp.bfloat16)
    return pick, place


def mixing_parts(out_ref, read_ref):
    mixing = jnp.dot(out_ref[...], read_ref[...], preferred_element_type=jnp.float32)
    high = mixing.astype(jnp.bfloat16)
    return high, (mixing - high.astype(jnp.float32)).astype(jnp.bfloat16)


def forward_kernel(
    sample_ref, embed_ref, gain_ref, proj_w_ref, out_ref, read_ref,
    normed_ref, proj_ref, prob_ref, pred_ref, *base_ref,
):
    embedded = jnp.dot(
        sample_ref[:, : embed_ref.shape[0]], embed_ref[...], preferred_element_type=jnp.float32
    ).astype(jnp.bfloat16)
    wide = embedded.astype(jnp.float32)
    mean = jnp.mean(wide, axis=1, keepdims=True)
    removed = wide - mean
    variance = jnp.mean(removed * removed, axis=1, keepdims=True)
    normed = (removed * lax.rsqrt(variance + NORM_EPSILON) * gain_ref[...]).astype(jnp.bfloat16)
    normed_ref[...] = normed
    proj_w = jnp.concatenate([proj_w_ref[i] for i in range(3)], axis=1)
    proj = jnp.dot(normed, proj_w, preferred_element_type=jnp.float32).astype(jnp.bfloat16)
    proj_ref[...] = proj
    attended = []
    for seq in range(sample_ref.shape[0] // SPD):
        rows = slice(seq * SPD, (seq + 1) * SPD)
        query, key, value = (proj[rows, i * HD : (i + 1) * HD] for i in range(3))
        scores = lax.dot_general(
            query, key, (((1,), (1,)), ((), ())), preferred_element_type=jnp.float32
        ) * (1.0 / math.sqrt(HD))
        raised = jnp.exp(scores - jnp.max(scores, axis=-1, keepdims=True))
        probs = raised / jnp.sum(raised, axis=-1, keepdims=True)
        prob_ref[rows, :] = probs
        attended.append(
            jnp.dot(
                probs.astype(jnp.bfloat16), value, preferred_element_type=jnp.float32
            ).astype(jnp.bfloat16)
        )
    attended = jnp.concatenate(attended, axis=0)
    high, low = mixing_parts(out_ref, read_ref)
    pred_ref[...] = jnp.dot(
        jnp.concatenate([attended, attended], axis=1),
        jnp.concatenate([high, low], axis=0),
        preferred_element_type=jnp.float32,
    ).astype(pred_ref.dtype)
    if base_ref:
        targets = sample_ref[:, embed_ref.shape[0] :].astype(jnp.float32)
        base_ref[0][...] = (
            jnp.dot(embedded, read_ref[...], preferred_element_type=jnp.float32) - targets
        )


def run_forward(samples, embed, gain, w_qkv, w_out, w_read, own):
    rows = samples.shape[0]
    kinds, model, head = w_qkv.shape
    out_width = w_read.shape[1]
    shapes = [
        jax.ShapeDtypeStruct((rows, model), jnp.bfloat16),
        jax.ShapeDtypeStruct((rows, kinds * head), jnp.bfloat16),
        jax.ShapeDtypeStruct((rows, SPD), jnp.float32),
        jax.ShapeDtypeStruct((rows, out_width), jnp.float32 if own else jnp.bfloat16),
    ]
    if own:
        shapes.append(jax.ShapeDtypeStruct((rows, out_width), jnp.float32))
    weights = (embed, gain, w_qkv, w_out, w_read)
    return pl.pallas_call(
        forward_kernel,
        out_shape=tuple(shapes),
        in_specs=[VMEM] * (1 + len(weights)),
        out_specs=(VMEM,) * len(shapes),
        compiler_params=pltpu.CompilerParams(vmem_limit_bytes=LIMIT),
        cost_estimate=pl.CostEstimate(
            flops=2 * rows * model * (embed.shape[0] + kinds * head),
            bytes_accessed=rows * model * 8,
            transcendentals=rows * SPD,
        ),
        name="forward_own" if own else "forward_other",
    )(samples, *weights)


def delta_kernel(share_ref, base_ref, delta_ref, *, scale):
    total = base_ref[...]
    for i in range(share_ref.shape[0]):
        total = total + share_ref[i].astype(jnp.float32)
    delta_ref[...] = (total * scale).astype(delta_ref.dtype)


def run_delta(shares, base, scale):
    return pl.pallas_call(
        functools.partial(delta_kernel, scale=scale),
        out_shape=jax.ShapeDtypeStruct(base.shape, jnp.bfloat16),
        in_specs=[VMEM, VMEM],
        out_specs=VMEM,
        compiler_params=pltpu.CompilerParams(vmem_limit_bytes=LIMIT),
        name="delta",
    )(shares, base)


def backward_kernel(delta_ref, out_ref, read_ref, proj_ref, prob_ref, normed_ref, *rest):
    start_ref = rest[0] if len(rest) == 2 else None
    grad_ref = rest[-1]
    across = (((1,), (1,)), ((), ()))
    down = (((0,), (0,)), ((), ()))
    delta = delta_ref[...]
    high, low = mixing_parts(out_ref, read_ref)
    grad_attended = lax.dot_general(
        jnp.concatenate([delta, delta], axis=1),
        jnp.concatenate([high, low], axis=1),
        across,
        preferred_element_type=jnp.float32,
    ).astype(jnp.bfloat16)
    grads = []
    for seq in range(delta_ref.shape[0] // SPD):
        rows = slice(seq * SPD, (seq + 1) * SPD)
        query, key, value = (proj_ref[rows, i * HD : (i + 1) * HD] for i in range(3))
        upper = grad_attended[rows]
        probs = prob_ref[rows, :]
        grad_probs = lax.dot_general(upper, value, across, preferred_element_type=jnp.float32)
        grad_value = lax.dot_general(
            probs.astype(jnp.bfloat16), upper, down, preferred_element_type=jnp.float32
        )
        inner = jnp.sum(probs * grad_probs, axis=-1, keepdims=True)
        grad_scores = (probs * (grad_probs - inner) * (1.0 / math.sqrt(HD))).astype(jnp.bfloat16)
        grad_query = jnp.dot(grad_scores, key, preferred_element_type=jnp.float32)
        grad_key = lax.dot_general(grad_scores, query, down, preferred_element_type=jnp.float32)
        grads.append(
            jnp.concatenate([grad_query, grad_key, grad_value], axis=1).astype(jnp.bfloat16)
        )
    grads = jnp.concatenate(grads, axis=0)

    total = lax.dot_general(normed_ref[...], grads, down, preferred_element_type=jnp.float32)
    if start_ref is None:
        grad_ref[...] = total
    else:
        total = total + start_ref[...]
        for i in range(grad_ref.shape[0]):
            grad_ref[i] = total[:, i * HD : (i + 1) * HD].astype(grad_ref.dtype)


def run_backward(delta, w_out, w_read, proj, prob, normed, start):
    rows, model = normed.shape
    heads = proj.shape[1]
    if start is None:
        out = jax.ShapeDtypeStruct((model, heads), jnp.float32)
    else:
        out = jax.ShapeDtypeStruct((heads // HD, model, HD), jnp.bfloat16)
    operands = [delta, w_out, w_read, proj, prob, normed]
    if start is not None:
        operands.append(start)
    return pl.pallas_call(
        backward_kernel,
        out_shape=out,
        in_specs=[VMEM] * len(operands),
        out_specs=VMEM,
        compiler_params=pltpu.CompilerParams(vmem_limit_bytes=LIMIT),
        cost_estimate=pl.CostEstimate(
            flops=2 * rows * model * heads, bytes_accessed=rows * model * 4, transcendentals=0
        ),
        name="backward_own" if start is None else "backward_other",
    )(*operands)


def split(values, rows):
    columns = 128
    high = values.astype(jnp.bfloat16)
    low = (values - high.astype(jnp.float32)).astype(jnp.bfloat16)
    both = jnp.stack([high, low], axis=-2)
    both = both.reshape(both.shape[:-2] + (-1, min(columns, both.shape[-1])))
    pad = [(0, 0)] * (both.ndim - 2)
    return jnp.pad(both, pad + [(0, rows - both.shape[-2]), (0, columns - both.shape[-1])])


def sum_over_devices(parts, gain):
    count_x, count_z = lax.axis_size("x"), lax.axis_size("z")
    shape, columns, width = parts.shape, parts.shape[-1], gain.shape[0]
    chunk = width // count_z
    spare = 8

    part = jnp.sum(swap(parts.reshape(count_x, -1, columns), "x").astype(jnp.float32), axis=0)
    for axis in ("core", "grp", "yhi"):
        gain = gain + swap_with(gain, axis)

    sent = jnp.concatenate(
        [
            part.astype(jnp.bfloat16).reshape(count_z, -1, columns),
            split(gain.reshape(count_z, chunk), spare),
        ],
        axis=1,
    )
    total = jnp.sum(swap(sent, "z").astype(jnp.float32), axis=0)
    rows = total.shape[0] - spare
    own_gain = total[rows, :chunk] + total[rows + 1, :chunk]
    sent = jnp.concatenate([total[:rows].astype(jnp.bfloat16), split(own_gain, spare)], axis=0)
    got = spread(sent, "z").reshape(count_z, -1, columns)
    gain = (
        got[:, rows, :chunk].astype(jnp.float32) + got[:, rows + 1, :chunk].astype(jnp.float32)
    ).reshape(width)
    gain_rows = 2 * width // columns
    sent = jnp.concatenate([got[:, :rows].reshape(-1, columns), split(gain, gain_rows)], axis=0)
    got = spread(sent, "x").reshape(count_x, -1, columns)
    gain = jnp.sum(got[:, -gain_rows:].astype(jnp.float32), axis=0)
    gain = (gain[: gain_rows // 2] + gain[gain_rows // 2 :]).reshape(width)
    return got[:, :-gain_rows].reshape(shape), gain


def shards(
    start_field,
    material,
    conductivity,
    owners,
    tile_ids,
    embed_weight,
    layer_norm_gain,
    w_qkv,
    w_out,
    w_read,
):
    gain_row = layer_norm_gain[None, :]
    final_local, send, place, embed = run_slab(
        start_field[0],
        material,
        conductivity[0],
        owners[0, 0, :, :, 0],
        tile_ids[0, 0],
        embed_weight,
    )
    send, embed = lax.optimization_barrier((send, embed))
    got = swap(send, SPACE)
    embed = jnp.stack([embed, swap_with(embed, "grp")])
    embed = jnp.stack([embed, swap_cores(embed)]).reshape((-1,) + embed_weight.shape)
    away = lax.axis_index(GROUP) ^ jnp.arange(embed.shape[0], dtype=jnp.int32)
    embed = embed[((away & 1) << 2) + ((away >> 2 & 1) << 1) + (away >> 1 & 1)]
    embed = embed.transpose(1, 0, 2).reshape(embed_weight.shape[0], -1)

    chips = lax.axis_size(CHIPS)
    copies = jnp.dot(
        jnp.tile(place, (chips, 1)), got, preferred_element_type=jnp.float32
    ).astype(jnp.bfloat16)
    copies, embed = lax.optimization_barrier((copies, embed))
    samples = swap(copies, CHIPS)

    samples_other = swap_cores(samples)
    weights = (embed, gain_row, w_qkv, w_out, w_read)
    normed, proj, prob, pred, base = run_forward(samples, *weights, own=True)
    normed_other, proj_other, prob_other, pred_other = run_forward(
        samples_other, *weights, own=False
    )
    chip_pred = (pred + swap_cores(pred_other).astype(jnp.float32)).astype(jnp.bfloat16)
    shares = spread(chip_pred, CHIPS).reshape((chips,) + base.shape)
    row_count = lax.axis_size(GROUP) * SPD
    loss_scale = math.sqrt(
        w_read.shape[0] / (lax.axis_size(SPACE) * row_count * w_read.shape[1])
    )
    delta = run_delta(shares, base, loss_scale)

    delta_other = swap_cores(delta)
    half = run_backward(delta, w_out, w_read, proj, prob, normed, None)
    grads = run_backward(
        delta_other, w_out, w_read, proj_other, prob_other, normed_other, half
    )

    gain_share = (
        jnp.sum(w_qkv.astype(jnp.float32) * grads.astype(jnp.float32), axis=(0, 2))
        / layer_norm_gain
    )
    weight_total, gain_total = sum_over_devices(grads, gain_share)
    return (final_local[None], weight_total, gain_total)


def solution(mesh):
    halves, space, members = (mesh.shape[name] for name in ("grp", "space", "mem"))
    fine = Mesh(
        mesh.devices.reshape(halves, space // 4, 4, members // 2, 2),
        ("grp", "z", "x", "yhi", "core"),
    )
    placed = (
        P(MEM, SPACE, "grp", None),
        P(SPACE, "grp", None),
        P(MEM, None),
        P(MEM, "grp", None, None, None),
        P(MEM, "grp", None, None),
        P(None, GROUP),
        P(),
        P(None, None, GROUP),
        P(GROUP, None),
        P(),
    )
    return jax.shard_map(
        shards,
        mesh=fine,
        in_specs=placed,
        out_specs=(P(MEM, SPACE, "grp", None), P(None, None, GROUP), P()),
        check_vma=False,
    )
```

```python
import functools
import math

import jax
import jax.numpy as jnp
from jax import lax
from jax.experimental import pallas as pl
from jax.experimental.pallas import tpu as pltpu
from jax.sharding import Mesh
from jax.sharding import PartitionSpec as P

SPD = 128
STEPS = 3
TILE = 16
HD = 128
NORM_EPSILON = 1e-06

SPACE = ("z", "x")
MEM = ("yhi", "core")
GROUP = ("grp", "yhi", "core")
CHIPS = ("grp", "yhi")

PAD = 4
VMEM = pl.BlockSpec(memory_space=pltpu.VMEM)
SMEM = pl.BlockSpec(memory_space=pltpu.SMEM)
LIMIT = 20 * 1024 * 1024
EXACT = lax.Precision.HIGHEST


def swap(parts, axis):
    return lax.all_to_all(parts, axis, split_axis=0, concat_axis=0, tiled=True)


def spread(own, axis):
    count = lax.axis_size(axis)
    return swap(jnp.broadcast_to(own[None], (count,) + own.shape), axis)


def swap_with(own, axis):
    return lax.ppermute(own, axis, [(0, 1), (1, 0)])


def swap_cores(own):
    return swap_with(own, "core")


def halos(field, material, width, beside):
    half = lax.axis_index("grp")

    def cut(span, axis):
        return jnp.stack(
            [
                lax.slice_in_dim(field, *span, axis=axis),
                lax.slice_in_dim(material, *span, axis=axis).astype(jnp.float32),
            ]
        )

    span_x, span_y = field.shape[:2]
    face = jnp.where(
        half == 0, cut((span_y - width, span_y), 1), cut((0, width), 1)
    )
    side = swap_with(face, "grp")
    side, beside = lax.optimization_barrier((side, beside))
    count = lax.axis_size(SPACE)
    forward = [(i, i + 1) for i in range(count - 1)]
    backward = [(i + 1, i) for i in range(count - 1)]
    top, bottom = side[:, -width:], side[:, :width]
    top = jnp.concatenate([top, cut((span_x - width, span_x), 0), top], axis=2)
    bottom = jnp.concatenate([bottom, cut((0, width), 0), bottom], axis=2)
    low = lax.ppermute(top, SPACE, forward)
    high = lax.ppermute(bottom, SPACE, backward)
    return side, low, high, beside


def over(first, last, body):
    for plane in range(first, last):
        body(plane)


def slab_kernel(
    place_ref,
    table_ref,
    field_ref,
    material_ref,
    side_ref,
    low_ref,
    high_ref,
    pick_ref,
    final_ref,
    send_ref,
    field_a,
    field_b,
    cond,
    coef,
    pairs,
    quads,
    rows_t,
    *,
    total_x,
    total_y,
):
    span_x, span_y, span_z = field_ref.shape
    width = low_ref.shape[1]
    rows = span_y + 2 * PAD
    planes = span_x + 2 * width
    own_x = slice(width, width + span_x)
    own_y = slice(PAD, PAD + span_y)
    ext_y = slice(PAD - width, PAD + span_y + width)

    field_a[...] = jnp.zeros_like(field_a)
    cond[...] = jnp.zeros_like(cond)
    for part, target in ((0, field_a), (1, cond)):
        target[own_x, slice(PAD - width, PAD), :] = side_ref[part]
        target[own_x, slice(PAD + span_y, PAD + span_y + width), :] = side_ref[part]
        target[slice(0, width), ext_y, :] = low_ref[part]
        target[slice(width + span_x, planes), ext_y, :] = high_ref[part]
    field_a[own_x, own_y, :] = field_ref[...]
    cond[own_x, own_y, :] = material_ref[...].astype(jnp.float32)

    place_x = place_ref[0] * span_x - width
    place_y = place_ref[1] * span_y - PAD
    row_id = place_y + lax.broadcasted_iota(jnp.int32, (rows, span_z), 0)
    col_id = lax.broadcasted_iota(jnp.int32, (rows, span_z), 1)
    inside_y = (row_id >= 0) & (row_id < total_y)
    first_z = col_id == 0
    last_z = col_id == span_z - 1

    def inside(plane):
        at = place_x + plane
        in_x = ((at >= 0) & (at < total_x)).astype(jnp.int32)
        return inside_y & (jnp.full((rows, span_z), in_x) > 0)

    def set_cond(plane):
        kind = cond[plane]
        value = jnp.zeros_like(kind)
        for level in range(table_ref.shape[0]):
            value = jnp.where(kind == float(level), table_ref[level], value)
        keep = inside(plane)
        cond[plane] = jnp.where(keep, value, 0.0)
        field_a[plane] = jnp.where(keep, field_a[plane], 0.0)

    over(0, planes, set_cond)

    def set_coef(plane):
        mine = 0.5 * cond[plane]
        keep = inside(plane)
        ups = mine + pltpu.roll(mine, 1, 0)
        downs = mine + pltpu.roll(mine, rows - 1, 0)
        before = mine + jnp.where(first_z, 0.0, pltpu.roll(mine, 1, 1))
        after = mine + jnp.where(last_z, 0.0, pltpu.roll(mine, span_z - 1, 1))
        left = mine + 0.5 * cond[plane - 1]
        right = mine + 0.5 * cond[plane + 1]
        rest = 1.0 - (ups + downs + before + after + left + right)
        coef[0, plane] = jnp.where(keep, rest, 0.0)
        coef[1, plane] = jnp.where(keep, left, 0.0)
        coef[2, plane] = jnp.where(keep, right, 0.0)
        coef[3, plane] = jnp.where(keep, ups, 0.0)
        coef[4, plane] = jnp.where(keep, downs, 0.0)
        coef[5, plane] = jnp.where(keep & ~first_z, before, 0.0)
        coef[6, plane] = jnp.where(keep & ~last_z, after, 0.0)

    over(1, planes - 1, set_coef)

    def step(source, target):
        def one(plane):
            mid = source[plane]
            value = coef[0, plane] * mid
            value = value + coef[1, plane] * source[plane - 1]
            value = value + coef[2, plane] * source[plane + 1]
            value = value + coef[3, plane] * pltpu.roll(mid, 1, 0)
            value = value + coef[4, plane] * pltpu.roll(mid, rows - 1, 0)
            value = value + coef[5, plane] * pltpu.roll(mid, 1, 1)
            value = value + coef[6, plane] * pltpu.roll(mid, span_z - 1, 1)
            target[plane] = value

        return one

    for number in range(STEPS):
        source, target = (field_a, field_b) if number % 2 == 0 else (field_b, field_a)
        over(1 + number, planes - 1 - number, step(source, target))

    before_last, last = (field_a, field_b) if STEPS % 2 == 1 else (field_b, field_a)
    final_ref[...] = last[own_x, own_y, :]

    for i in range(span_x // 2):
        plane = width + 2 * i
        pairs[span_y * i : span_y * (i + 1), :] = (
            before_last[plane, own_y, :] + before_last[plane + 1, own_y, :]
        )
    for i in range(span_x // 4):
        plane = width + 4 * i
        quads[span_y * i : span_y * (i + 1), :] = (
            last[plane, own_y, :] + last[plane + 1, own_y, :]
        ) + (last[plane + 2, own_y, :] + last[plane + 3, own_y, :])
    depth = TILE // 2
    tiles = span_z // TILE
    z_id = lax.broadcasted_iota(jnp.int32, (span_z, depth * tiles), 0) // 2
    c_id = lax.broadcasted_iota(jnp.int32, (span_z, depth * tiles), 1)
    fold_z = (z_id == (c_id % tiles) * depth + c_id // tiles).astype(jnp.float32)

    def fold_y(stacked, group):
        size = stacked.shape[0]
        out_id = lax.broadcasted_iota(jnp.int32, (size // group, size), 0)
        in_id = lax.broadcasted_iota(jnp.int32, (size // group, size), 1)
        matrix = (out_id == in_id // group).astype(jnp.float32)
        part = jnp.dot(stacked, fold_z, precision=EXACT, preferred_element_type=jnp.float32)
        return jnp.dot(matrix, part, precision=EXACT, preferred_element_type=jnp.float32)

    fine = fold_y(pairs[...], 2) * 0.125
    rough = fold_y(quads[...], 4) * 0.03125
    fine_rows, rough_rows = fine.shape[0], rough.shape[0]
    for k in range(depth):
        cut = slice(tiles * k, tiles * (k + 1))
        rows_t[pl.ds(k, fine_rows, stride=depth), :] = fine[:, cut]
        rows_t[pl.ds(fine_rows * depth + k, rough_rows, stride=depth), :] = rough[:, cut]
    send_ref[...] = lax.dot_general(
        pick_ref[...],
        rows_t[...].astype(jnp.bfloat16),
        (((1,), (1,)), ((), ())),
        preferred_element_type=jnp.float32,
    ).astype(jnp.bfloat16)


def run_slab(field, material, table, owner_list, tile_list, embed_own):
    pick, place = slots(owner_list, tile_list, field.shape[2] // TILE)
    side, low, high, embed_own = halos(field, material, STEPS, embed_own)
    embed = jnp.stack([embed_own, swap_with(embed_own, "yhi")])
    origin = jnp.stack([lax.axis_index(SPACE), lax.axis_index("grp")]).astype(jnp.int32)
    totals = (lax.axis_size(SPACE) * field.shape[0], lax.axis_size("grp") * field.shape[1])
    final, send = call_slab(origin, table, field, material, side, low, high, pick, totals)
    return final, send, place, embed


def call_slab(origin, table, field, material, side, low, high, pick, totals):
    span_x, span_y, span_z = field.shape
    planes, rows = span_x + 2 * low.shape[1], span_y + 2 * PAD
    tiles = span_z // TILE
    values = (span_x * span_y // 4 + span_x * span_y // 16) * TILE // 2
    extended = pltpu.VMEM((planes, rows, span_z), jnp.float32)
    return pl.pallas_call(
        functools.partial(slab_kernel, total_x=totals[0], total_y=totals[1]),
        out_shape=(
            jax.ShapeDtypeStruct(field.shape, jnp.float32),
            jax.ShapeDtypeStruct((pick.shape[0], values), jnp.bfloat16),
        ),
        in_specs=[SMEM, SMEM] + [VMEM] * 6,
        out_specs=(VMEM, VMEM),
        scratch_shapes=[
            extended,
            extended,
            extended,
            pltpu.VMEM((7, planes, rows, span_z), jnp.float32),
            pltpu.VMEM((span_x * span_y // 2, span_z), jnp.float32),
            pltpu.VMEM((span_x * span_y // 4, span_z), jnp.float32),
            pltpu.VMEM((values, tiles), jnp.float32),
        ],
        compiler_params=pltpu.CompilerParams(vmem_limit_bytes=LIMIT),
        name="slab",
    )(origin, table, field, material, side, low, high, pick)


def slots(owner_list, tile_list, tile_count):
    shard_count, slot_count = owner_list.shape
    capacity = 2 * slot_count // shard_count
    my_index = lax.axis_index(SPACE)
    slot_order = jnp.arange(slot_count, dtype=jnp.int32)
    earlier = slot_order[:, None] < slot_order[None, :]
    owned_here = owner_list == my_index
    here_rank = jnp.dot(
        owned_here.astype(jnp.bfloat16),
        earlier.astype(jnp.bfloat16),
        preferred_element_type=jnp.float32,
    ).astype(jnp.int32)
    slot_ids = jnp.arange(capacity, dtype=jnp.int32)
    slot_match = owned_here[:, None, :] & (here_rank[:, None, :] == slot_ids[None, :, None])
    chosen = jnp.sum(jnp.where(slot_match, tile_list[:, None, :] + 1, 0), axis=2) - 1
    tile_ids = jnp.arange(tile_count, dtype=jnp.int32)
    pick = (chosen.reshape(-1, 1) == tile_ids[None, :]).astype(jnp.bfloat16)
    own_owner = jnp.take(owner_list, my_index, axis=0)
    same_owner = own_owner[:, None] == own_owner[None, :]
    own_rank = jnp.sum((same_owner & earlier).astype(jnp.int32), axis=0)
    flat_index = own_owner * capacity + own_rank
    flat_ids = jnp.arange(shard_count * capacity, dtype=jnp.int32)
    place = (flat_index[:, None] == flat_ids[None, :]).astype(jnp.bfloat16)
    return pick, place


def layout(token_width, model):
    heads = 6 * HD
    mix = model + model // token_width * heads
    return heads, mix, mix + HD, mix + 2 * HD


def prepare_kernel(
    order_ref, parts_ref, w_own_ref, w_other_ref, out_own_ref, out_other_ref, read_ref, all_ref
):
    count, width, rows = parts_ref.shape
    model = count * width
    heads, mix, read, _ = layout(rows, model)
    for i in range(count // 2):
        pair = jnp.concatenate(
            [parts_ref[order_ref[2 * i]], parts_ref[order_ref[2 * i + 1]]], axis=0
        )
        all_ref[:, 2 * i * width : 2 * (i + 1) * width] = pair.T
    for block in range(model // rows):
        for head, ref in enumerate((w_own_ref, w_other_ref)):
            for i in range(3):
                start = model + block * heads + (3 * head + i) * HD
                all_ref[:, start : start + HD] = ref[i, block * rows : (block + 1) * rows, :]
    out_w = jnp.concatenate([out_own_ref[...], out_other_ref[...]], axis=0)
    mixing = jnp.dot(out_w, read_ref[...], preferred_element_type=jnp.float32)
    high = mixing.astype(jnp.bfloat16)
    all_ref[: 2 * HD, mix:read] = high
    all_ref[2 * HD :, mix:read] = (mixing - high.astype(jnp.float32)).astype(jnp.bfloat16)
    share = 2 * width
    start = pl.multiple_of(order_ref[count] * share, share)
    all_ref[:share, read:] = read_ref[pl.ds(start, share), :]
    all_ref[share:, read:] = jnp.zeros((rows - share, HD), jnp.bfloat16)


def run_prepare(order, parts, w_own, w_other, out_own, out_other, w_read):
    rows, model = parts.shape[2], w_own.shape[1]
    return pl.pallas_call(
        prepare_kernel,
        out_shape=jax.ShapeDtypeStruct((rows, layout(rows, model)[-1]), jnp.bfloat16),
        in_specs=[SMEM] + [VMEM] * 6,
        out_specs=VMEM,
        compiler_params=pltpu.CompilerParams(vmem_limit_bytes=LIMIT),
        cost_estimate=pl.CostEstimate(flops=1 << 28, bytes_accessed=1 << 23, transcendentals=0),
        name="prepare",
    )(order, parts, w_own, w_other, out_own, out_other, w_read)


def forward_kernel(
    chip_ref, sample_ref, all_ref, gain_ref, normed_ref, proj_ref, prob_ref, pred_ref, embed_ref
):
    token_width = all_ref.shape[0]
    model = normed_ref.shape[1]
    heads, mix, read, _ = layout(token_width, model)
    across = (((1,), (1,)), ((), ()))
    embedded = jnp.dot(
        sample_ref[:, :token_width], all_ref[:, :model], preferred_element_type=jnp.float32
    ).astype(jnp.bfloat16)
    embed_ref[...] = embedded
    wide = embedded.astype(jnp.float32)
    mean = jnp.mean(wide, axis=1, keepdims=True)
    removed = wide - mean
    variance = jnp.mean(removed * removed, axis=1, keepdims=True)
    normed = (removed * lax.rsqrt(variance + NORM_EPSILON) * gain_ref[...]).astype(jnp.bfloat16)
    normed_ref[...] = normed
    proj_w = jnp.concatenate(
        [all_ref[:, start : start + heads] for start in range(model, mix, heads)], axis=0
    )
    proj = jnp.dot(normed, proj_w, preferred_element_type=jnp.float32).astype(jnp.bfloat16)
    proj_ref[...] = proj
    attended = []
    for seq in range(sample_ref.shape[0] // SPD):
        rows = slice(seq * SPD, (seq + 1) * SPD)
        parts = []
        for head in range(2):
            query, key, value = (
                proj[rows, i * HD : (i + 1) * HD] for i in range(3 * head, 3 * head + 3)
            )
            scores = lax.dot_general(
                query, key, across, preferred_element_type=jnp.float32
            ) * (1.0 / math.sqrt(HD))
            raised = jnp.exp(scores - jnp.max(scores, axis=-1, keepdims=True))
            probs = raised / jnp.sum(raised, axis=-1, keepdims=True)
            prob_ref[rows, head * SPD : (head + 1) * SPD] = probs
            parts.append(
                jnp.dot(
                    probs.astype(jnp.bfloat16), value, preferred_element_type=jnp.float32
                ).astype(jnp.bfloat16)
            )
        attended.append(jnp.concatenate(parts, axis=1))
    attended = jnp.concatenate(attended, axis=0)
    share = model // 4
    start = pl.multiple_of(chip_ref[0] * share, share)
    pred_ref[...] = jnp.dot(
        jnp.concatenate([attended, attended, embed_ref[:, pl.ds(start, share)]], axis=1),
        jnp.concatenate([all_ref[:, mix:read], all_ref[:share, read:]], axis=0),
        preferred_element_type=jnp.float32,
    ).astype(pred_ref.dtype)


def run_forward(chip, samples, weights, gain):
    rows = samples.shape[0]
    model = gain.shape[1]
    heads = layout(weights.shape[0], model)[0]
    shapes = (
        jax.ShapeDtypeStruct((rows, model), jnp.bfloat16),
        jax.ShapeDtypeStruct((rows, heads), jnp.bfloat16),
        jax.ShapeDtypeStruct((rows, 2 * SPD), jnp.float32),
        jax.ShapeDtypeStruct((rows, HD), jnp.bfloat16),
    )
    return pl.pallas_call(
        forward_kernel,
        out_shape=shapes,
        in_specs=[SMEM] + [VMEM] * 3,
        out_specs=(VMEM,) * len(shapes),
        scratch_shapes=[pltpu.VMEM((rows, model), jnp.bfloat16)],
        compiler_params=pltpu.CompilerParams(vmem_limit_bytes=LIMIT),
        cost_estimate=pl.CostEstimate(
            flops=2 * rows * model * (weights.shape[0] + heads),
            bytes_accessed=rows * model * 8,
            transcendentals=2 * rows * SPD,
        ),
        name="forward",
    )(chip, samples, weights, gain)


def delta_kernel(share_ref, sample_ref, delta_ref, *, scale):
    targets = sample_ref[:, sample_ref.shape[1] - delta_ref.shape[1] :]
    total = share_ref[0].astype(jnp.float32)
    for i in range(1, share_ref.shape[0]):
        total = total + share_ref[i].astype(jnp.float32)
    delta_ref[...] = ((total - targets.astype(jnp.float32)) * scale).astype(delta_ref.dtype)


def run_delta(shares, samples, scale):
    return pl.pallas_call(
        functools.partial(delta_kernel, scale=scale),
        out_shape=jax.ShapeDtypeStruct(shares.shape[1:], jnp.bfloat16),
        in_specs=[VMEM, VMEM],
        out_specs=VMEM,
        compiler_params=pltpu.CompilerParams(vmem_limit_bytes=LIMIT),
        name="delta",
    )(shares, samples)


def backward_kernel(
    delta_ref, all_ref, proj_ref, prob_ref, normed_ref, grad_ref, *, head
):
    _, mix, read, _ = layout(all_ref.shape[0], normed_ref.shape[1])
    across = (((1,), (1,)), ((), ()))
    down = (((0,), (0,)), ((), ()))
    delta = delta_ref[...]
    mixing = [all_ref[(2 * i + head) * HD : (2 * i + head + 1) * HD, mix:read] for i in range(2)]
    grad_attended = lax.dot_general(
        jnp.concatenate([delta, delta], axis=1),
        jnp.concatenate(mixing, axis=1),
        across,
        preferred_element_type=jnp.float32,
    ).astype(jnp.bfloat16)
    grads = []
    for seq in range(delta_ref.shape[0] // SPD):
        rows = slice(seq * SPD, (seq + 1) * SPD)
        query, key, value = (
            proj_ref[rows, i * HD : (i + 1) * HD] for i in range(3 * head, 3 * head + 3)
        )
        upper = grad_attended[rows]
        probs = prob_ref[rows, head * SPD : (head + 1) * SPD]
        grad_probs = lax.dot_general(upper, value, across, preferred_element_type=jnp.float32)
        grad_value = lax.dot_general(
            probs.astype(jnp.bfloat16), upper, down, preferred_element_type=jnp.float32
        )
        inner = jnp.sum(probs * grad_probs, axis=-1, keepdims=True)
        grad_scores = (probs * (grad_probs - inner) * (1.0 / math.sqrt(HD))).astype(jnp.bfloat16)
        grad_query = jnp.dot(grad_scores, key, preferred_element_type=jnp.float32)
        grad_key = lax.dot_general(grad_scores, query, down, preferred_element_type=jnp.float32)
        grads.append(
            jnp.concatenate([grad_query, grad_key, grad_value], axis=1).astype(jnp.bfloat16)
        )
    grads = jnp.concatenate(grads, axis=0)
    total = lax.dot_general(normed_ref[...], grads, down, preferred_element_type=jnp.float32)
    for i in range(grad_ref.shape[0]):
        grad_ref[i] = total[:, i * HD : (i + 1) * HD].astype(grad_ref.dtype)


def run_backward(delta, weights, proj, prob, normed, head):
    rows, model = normed.shape
    heads = proj.shape[1] // 2
    operands = (delta, weights, proj, prob, normed)
    return pl.pallas_call(
        functools.partial(backward_kernel, head=head),
        out_shape=jax.ShapeDtypeStruct((heads // HD, model, HD), jnp.bfloat16),
        in_specs=[VMEM] * len(operands),
        out_specs=VMEM,
        compiler_params=pltpu.CompilerParams(vmem_limit_bytes=LIMIT),
        cost_estimate=pl.CostEstimate(
            flops=2 * rows * model * heads, bytes_accessed=rows * model * 4, transcendentals=0
        ),
        name="backward_other" if head else "backward_own",
    )(*operands)


def sum_over_devices(parts, gain):
    count_x, count_z = lax.axis_size("x"), lax.axis_size("z")
    shape, columns, width = parts.shape, parts.shape[-1], gain.shape[0]

    sent = jnp.concatenate(
        [
            parts.reshape(count_x, -1, columns),
            gain.astype(jnp.bfloat16).reshape(count_x, -1, columns),
        ],
        axis=1,
    )
    extra = width // (count_x * columns)
    part = jnp.sum(swap(sent, "x").astype(jnp.float32), axis=0)
    gain = part[-extra:]
    part = part[:-extra].astype(jnp.bfloat16).reshape(count_z, -1, columns)
    total = jnp.sum(swap(part, "z").astype(jnp.float32), axis=0).astype(jnp.bfloat16)
    for axis in ("core", "grp", "yhi"):
        gain = gain + swap_with(gain, axis)

    sent = jnp.concatenate([total, gain.astype(jnp.bfloat16)], axis=0)
    got = spread(sent, "z").reshape(count_z, -1, columns)
    gain = jnp.sum(got[:, -extra:].astype(jnp.float32), axis=0)
    sent = jnp.concatenate([got[:, :-extra].reshape(-1, columns), gain.astype(jnp.bfloat16)], axis=0)
    got = spread(sent, "x").reshape(count_x, -1, columns)
    gain = got[:, -extra:].astype(jnp.float32)
    return got[:, :-extra].reshape(shape), gain.reshape(width)


def shards(
    start_field,
    material,
    conductivity,
    owners,
    tile_ids,
    embed_weight,
    layer_norm_gain,
    w_qkv,
    w_out,
    w_read,
):
    gain_row = layer_norm_gain[None, :]
    final_local, send, place, embed = run_slab(
        start_field[0],
        material,
        conductivity[0],
        owners[0, 0, :, :, 0],
        tile_ids[0, 0],
        embed_weight.T,
    )
    send, embed = lax.optimization_barrier((send, embed))
    got = swap(send.reshape(lax.axis_size(SPACE), -1, send.shape[1]), SPACE)
    embed = jnp.stack([embed, swap_with(embed, "grp")])
    embed, w_own, out_own = lax.optimization_barrier((embed, w_qkv, w_out))
    w_other, out_other = swap_cores(w_own), swap_cores(out_own)
    embed = jnp.stack([embed, swap_cores(embed)]).reshape((-1,) + embed_weight.T.shape)
    away = lax.axis_index(GROUP) ^ jnp.arange(embed.shape[0], dtype=jnp.int32)
    order = ((away & 1) << 2) + ((away >> 2 & 1) << 1) + (away >> 1 & 1)

    chip = lax.axis_index(CHIPS).astype(jnp.int32)[None]
    order = jnp.concatenate([order, chip])
    weights = run_prepare(order, embed, w_own, w_other, out_own, out_other, w_read)
    got, weights, gain_row = lax.optimization_barrier((got, weights, gain_row))
    got = got.reshape(-1, got.shape[2])

    chips = lax.axis_size(CHIPS)
    copies = jnp.dot(
        jnp.tile(place, (chips, 1)), got, preferred_element_type=jnp.float32
    ).astype(jnp.bfloat16)
    samples = swap(copies, CHIPS)

    normed, proj, prob, pred = run_forward(chip, samples, weights, gain_row)
    shares = spread(pred, CHIPS).reshape((chips,) + pred.shape)
    row_count = lax.axis_size(GROUP) * SPD
    loss_scale = math.sqrt(
        w_read.shape[0] / (lax.axis_size(SPACE) * row_count * w_read.shape[1])
    )
    delta = run_delta(shares, samples, loss_scale)

    saved = (weights, proj, prob, normed)
    grads_other = swap_cores(run_backward(delta, *saved, head=1))
    grads = (
        run_backward(delta, *saved, head=0).astype(jnp.float32) + grads_other.astype(jnp.float32)
    ).astype(jnp.bfloat16)

    gain_share = (
        jnp.sum(w_qkv.astype(jnp.float32) * grads.astype(jnp.float32), axis=(0, 2))
        / layer_norm_gain
    )
    weight_total, gain_total = sum_over_devices(grads, gain_share)
    return (final_local[None], weight_total, gain_total)


def solution(mesh):
    halves, space, members = (mesh.shape[name] for name in ("grp", "space", "mem"))
    fine = Mesh(
        mesh.devices.reshape(halves, space // 4, 4, members // 2, 2),
        ("grp", "z", "x", "yhi", "core"),
    )
    placed = (
        P(MEM, SPACE, "grp", None),
        P(SPACE, "grp", None),
        P(MEM, None),
        P(MEM, "grp", None, None, None),
        P(MEM, "grp", None, None),
        P(None, GROUP),
        P(),
        P(None, None, GROUP),
        P(GROUP, None),
        P(),
    )
    return jax.shard_map(
        shards,
        mesh=fine,
        in_specs=placed,
        out_specs=(P(MEM, SPACE, "grp", None), P(None, None, GROUP), P()),
        check_vma=False,
    )
```

```python
import functools
import math

import jax
import jax.numpy as jnp
from jax import lax
from jax.experimental import pallas as pl
from jax.experimental.pallas import tpu as pltpu
from jax.sharding import Mesh
from jax.sharding import PartitionSpec as P

SPD = 128
STEPS = 3
TILE = 16
HD = 128
NORM_EPSILON = 1e-06

SPACE = ("z", "x")
MEM = ("yhi", "core")
GROUP = ("grp", "yhi", "core")
CHIPS = ("grp", "yhi")

PAD = 4
VMEM = pl.BlockSpec(memory_space=pltpu.VMEM)
SMEM = pl.BlockSpec(memory_space=pltpu.SMEM)
LIMIT = 20 * 1024 * 1024
FORWARD_LIMIT = 48 * 1024 * 1024
EXACT = lax.Precision.HIGHEST


def swap(parts, axis):
    return lax.all_to_all(parts, axis, split_axis=0, concat_axis=0, tiled=True)


def spread(own, axis):
    count = lax.axis_size(axis)
    return swap(jnp.broadcast_to(own[None], (count,) + own.shape), axis)


def swap_with(own, axis):
    return lax.ppermute(own, axis, [(0, 1), (1, 0)])


def swap_cores(own):
    return swap_with(own, "core")


def halos(field, material, width, beside):
    half = lax.axis_index("grp")

    def cut(span, axis):
        return jnp.stack(
            [
                lax.slice_in_dim(field, *span, axis=axis),
                lax.slice_in_dim(material, *span, axis=axis).astype(jnp.float32),
            ]
        )

    span_x, span_y = field.shape[:2]
    face = jnp.where(
        half == 0, cut((span_y - width, span_y), 1), cut((0, width), 1)
    )
    side = swap_with(face, "grp")
    side, beside = lax.optimization_barrier((side, beside))
    count = lax.axis_size(SPACE)
    forward = [(i, i + 1) for i in range(count - 1)]
    backward = [(i + 1, i) for i in range(count - 1)]
    top, bottom = side[:, -width:], side[:, :width]
    top = jnp.concatenate([top, cut((span_x - width, span_x), 0), top], axis=2)
    bottom = jnp.concatenate([bottom, cut((0, width), 0), bottom], axis=2)
    low = lax.ppermute(top, SPACE, forward)
    high = lax.ppermute(bottom, SPACE, backward)
    return side, low, high, beside


def over(first, last, body):
    for plane in range(first, last):
        body(plane)


def slab_kernel(
    place_ref,
    table_ref,
    field_ref,
    material_ref,
    side_ref,
    low_ref,
    high_ref,
    pick_ref,
    final_ref,
    send_ref,
    field_a,
    field_b,
    cond,
    coef,
    pairs,
    quads,
    rows_t,
    *,
    total_x,
    total_y,
):
    span_x, span_y, span_z = field_ref.shape
    width = low_ref.shape[1]
    rows = span_y + 2 * PAD
    planes = span_x + 2 * width
    own_x = slice(width, width + span_x)
    own_y = slice(PAD, PAD + span_y)
    ext_y = slice(PAD - width, PAD + span_y + width)

    field_a[...] = jnp.zeros_like(field_a)
    cond[...] = jnp.zeros_like(cond)
    for part, target in ((0, field_a), (1, cond)):
        target[own_x, slice(PAD - width, PAD), :] = side_ref[part]
        target[own_x, slice(PAD + span_y, PAD + span_y + width), :] = side_ref[part]
        target[slice(0, width), ext_y, :] = low_ref[part]
        target[slice(width + span_x, planes), ext_y, :] = high_ref[part]
    field_a[own_x, own_y, :] = field_ref[...]
    cond[own_x, own_y, :] = material_ref[...].astype(jnp.float32)

    place_x = place_ref[0] * span_x - width
    place_y = place_ref[1] * span_y - PAD
    row_id = place_y + lax.broadcasted_iota(jnp.int32, (rows, span_z), 0)
    col_id = lax.broadcasted_iota(jnp.int32, (rows, span_z), 1)
    inside_y = (row_id >= 0) & (row_id < total_y)
    first_z = col_id == 0
    last_z = col_id == span_z - 1

    def inside(plane):
        at = place_x + plane
        in_x = ((at >= 0) & (at < total_x)).astype(jnp.int32)
        return inside_y & (jnp.full((rows, span_z), in_x) > 0)

    def set_cond(plane):
        kind = cond[plane]
        value = jnp.zeros_like(kind)
        for level in range(table_ref.shape[0]):
            value = jnp.where(kind == float(level), table_ref[level], value)
        keep = inside(plane)
        cond[plane] = jnp.where(keep, value, 0.0)
        field_a[plane] = jnp.where(keep, field_a[plane], 0.0)

    over(0, planes, set_cond)

    def set_coef(plane):
        mine = 0.5 * cond[plane]
        keep = inside(plane)
        ups = mine + pltpu.roll(mine, 1, 0)
        downs = mine + pltpu.roll(mine, rows - 1, 0)
        before = mine + jnp.where(first_z, 0.0, pltpu.roll(mine, 1, 1))
        after = mine + jnp.where(last_z, 0.0, pltpu.roll(mine, span_z - 1, 1))
        left = mine + 0.5 * cond[plane - 1]
        right = mine + 0.5 * cond[plane + 1]
        rest = 1.0 - (ups + downs + before + after + left + right)
        coef[0, plane] = jnp.where(keep, rest, 0.0)
        coef[1, plane] = jnp.where(keep, left, 0.0)
        coef[2, plane] = jnp.where(keep, right, 0.0)
        coef[3, plane] = jnp.where(keep, ups, 0.0)
        coef[4, plane] = jnp.where(keep, downs, 0.0)
        coef[5, plane] = jnp.where(keep & ~first_z, before, 0.0)
        coef[6, plane] = jnp.where(keep & ~last_z, after, 0.0)

    over(1, planes - 1, set_coef)

    def step(source, target):
        def one(plane):
            mid = source[plane]
            value = coef[0, plane] * mid
            value = value + coef[1, plane] * source[plane - 1]
            value = value + coef[2, plane] * source[plane + 1]
            value = value + coef[3, plane] * pltpu.roll(mid, 1, 0)
            value = value + coef[4, plane] * pltpu.roll(mid, rows - 1, 0)
            value = value + coef[5, plane] * pltpu.roll(mid, 1, 1)
            value = value + coef[6, plane] * pltpu.roll(mid, span_z - 1, 1)
            target[plane] = value

        return one

    for number in range(STEPS):
        source, target = (field_a, field_b) if number % 2 == 0 else (field_b, field_a)
        over(1 + number, planes - 1 - number, step(source, target))

    before_last, last = (field_a, field_b) if STEPS % 2 == 1 else (field_b, field_a)
    final_ref[...] = last[own_x, own_y, :]

    for i in range(span_x // 2):
        plane = width + 2 * i
        pairs[span_y * i : span_y * (i + 1), :] = (
            before_last[plane, own_y, :] + before_last[plane + 1, own_y, :]
        )
    for i in range(span_x // 4):
        plane = width + 4 * i
        quads[span_y * i : span_y * (i + 1), :] = (
            last[plane, own_y, :] + last[plane + 1, own_y, :]
        ) + (last[plane + 2, own_y, :] + last[plane + 3, own_y, :])
    depth = TILE // 2
    tiles = span_z // TILE
    z_id = lax.broadcasted_iota(jnp.int32, (span_z, depth * tiles), 0) // 2
    c_id = lax.broadcasted_iota(jnp.int32, (span_z, depth * tiles), 1)
    fold_z = (z_id == (c_id % tiles) * depth + c_id // tiles).astype(jnp.float32)

    def fold_y(stacked, group):
        size = stacked.shape[0]
        out_id = lax.broadcasted_iota(jnp.int32, (size // group, size), 0)
        in_id = lax.broadcasted_iota(jnp.int32, (size // group, size), 1)
        matrix = (out_id == in_id // group).astype(jnp.float32)
        part = jnp.dot(stacked, fold_z, precision=EXACT, preferred_element_type=jnp.float32)
        return jnp.dot(matrix, part, precision=EXACT, preferred_element_type=jnp.float32)

    fine = fold_y(pairs[...], 2) * 0.125
    rough = fold_y(quads[...], 4) * 0.03125
    fine_rows, rough_rows = fine.shape[0], rough.shape[0]
    for k in range(depth):
        cut = slice(tiles * k, tiles * (k + 1))
        rows_t[pl.ds(k, fine_rows, stride=depth), :] = fine[:, cut]
        rows_t[pl.ds(fine_rows * depth + k, rough_rows, stride=depth), :] = rough[:, cut]
    send_ref[...] = lax.dot_general(
        pick_ref[...],
        rows_t[...].astype(jnp.bfloat16),
        (((1,), (1,)), ((), ())),
        preferred_element_type=jnp.float32,
    ).astype(jnp.bfloat16)


def run_slab(field, material, table, owner_list, tile_list, embed_own):
    pick, place = slots(owner_list, tile_list, field.shape[2] // TILE)
    side, low, high, embed_own = halos(field, material, STEPS, embed_own)
    embed = jnp.stack([embed_own, swap_with(embed_own, "yhi")])
    origin = jnp.stack([lax.axis_index(SPACE), lax.axis_index("grp")]).astype(jnp.int32)
    totals = (lax.axis_size(SPACE) * field.shape[0], lax.axis_size("grp") * field.shape[1])
    final, send = call_slab(origin, table, field, material, side, low, high, pick, totals)
    return final, send, place, embed


def call_slab(origin, table, field, material, side, low, high, pick, totals):
    span_x, span_y, span_z = field.shape
    planes, rows = span_x + 2 * low.shape[1], span_y + 2 * PAD
    tiles = span_z // TILE
    values = (span_x * span_y // 4 + span_x * span_y // 16) * TILE // 2
    extended = pltpu.VMEM((planes, rows, span_z), jnp.float32)
    return pl.pallas_call(
        functools.partial(slab_kernel, total_x=totals[0], total_y=totals[1]),
        out_shape=(
            jax.ShapeDtypeStruct(field.shape, jnp.float32),
            jax.ShapeDtypeStruct((pick.shape[0], values), jnp.bfloat16),
        ),
        in_specs=[SMEM, SMEM] + [VMEM] * 6,
        out_specs=(VMEM, VMEM),
        scratch_shapes=[
            extended,
            extended,
            extended,
            pltpu.VMEM((7, planes, rows, span_z), jnp.float32),
            pltpu.VMEM((span_x * span_y // 2, span_z), jnp.float32),
            pltpu.VMEM((span_x * span_y // 4, span_z), jnp.float32),
            pltpu.VMEM((values, tiles), jnp.float32),
        ],
        compiler_params=pltpu.CompilerParams(vmem_limit_bytes=LIMIT),
        name="slab",
    )(origin, table, field, material, side, low, high, pick)


def slots(owner_list, tile_list, tile_count):
    shard_count, slot_count = owner_list.shape
    capacity = 2 * slot_count // shard_count
    my_index = lax.axis_index(SPACE)
    slot_order = jnp.arange(slot_count, dtype=jnp.int32)
    earlier = slot_order[:, None] < slot_order[None, :]
    owned_here = owner_list == my_index
    here_rank = jnp.dot(
        owned_here.astype(jnp.bfloat16),
        earlier.astype(jnp.bfloat16),
        preferred_element_type=jnp.float32,
    ).astype(jnp.int32)
    slot_ids = jnp.arange(capacity, dtype=jnp.int32)
    slot_match = owned_here[:, None, :] & (here_rank[:, None, :] == slot_ids[None, :, None])
    chosen = jnp.sum(jnp.where(slot_match, tile_list[:, None, :] + 1, 0), axis=2) - 1
    tile_ids = jnp.arange(tile_count, dtype=jnp.int32)
    pick = (chosen.reshape(-1, 1) == tile_ids[None, :]).astype(jnp.bfloat16)
    own_owner = jnp.take(owner_list, my_index, axis=0)
    same_owner = own_owner[:, None] == own_owner[None, :]
    own_rank = jnp.sum((same_owner & earlier).astype(jnp.int32), axis=0)
    flat_index = own_owner * capacity + own_rank
    flat_ids = jnp.arange(shard_count * capacity, dtype=jnp.int32)
    place = (flat_index[:, None] == flat_ids[None, :]).astype(jnp.bfloat16)
    return pick, place


def layout(token_width, model):
    heads = 6 * HD
    mix = model + model // token_width * heads
    return heads, mix, mix + HD, mix + 2 * HD


def prepare_kernel(
    order_ref, parts_ref, w_own_ref, w_other_ref, out_own_ref, out_other_ref, read_ref, all_ref
):
    count, width, rows = parts_ref.shape
    model = count * width
    heads, mix, read, _ = layout(rows, model)
    for i in range(count // 2):
        pair = jnp.concatenate(
            [parts_ref[order_ref[2 * i]], parts_ref[order_ref[2 * i + 1]]], axis=0
        )
        all_ref[:, 2 * i * width : 2 * (i + 1) * width] = pair.T
    for block in range(model // rows):
        for head, ref in enumerate((w_own_ref, w_other_ref)):
            for i in range(3):
                start = model + block * heads + (3 * head + i) * HD
                all_ref[:, start : start + HD] = ref[i, block * rows : (block + 1) * rows, :]
    out_w = jnp.concatenate([out_own_ref[...], out_other_ref[...]], axis=0)
    mixing = jnp.dot(out_w, read_ref[...], preferred_element_type=jnp.float32)
    high = mixing.astype(jnp.bfloat16)
    all_ref[: 2 * HD, mix:read] = high
    all_ref[2 * HD :, mix:read] = (mixing - high.astype(jnp.float32)).astype(jnp.bfloat16)
    share = 2 * width
    start = pl.multiple_of(order_ref[count] * share, share)
    all_ref[:share, read:] = read_ref[pl.ds(start, share), :]
    all_ref[share:, read:] = jnp.zeros((rows - share, HD), jnp.bfloat16)


def run_prepare(order, parts, w_own, w_other, out_own, out_other, w_read):
    rows, model = parts.shape[2], w_own.shape[1]
    return pl.pallas_call(
        prepare_kernel,
        out_shape=jax.ShapeDtypeStruct((rows, layout(rows, model)[-1]), jnp.bfloat16),
        in_specs=[SMEM] + [VMEM] * 6,
        out_specs=VMEM,
        compiler_params=pltpu.CompilerParams(vmem_limit_bytes=LIMIT),
        cost_estimate=pl.CostEstimate(flops=1 << 28, bytes_accessed=1 << 23, transcendentals=0),
        name="prepare",
    )(order, parts, w_own, w_other, out_own, out_other, w_read)


def forward_kernel(
    chip_ref, sample_ref, all_hbm, gain_ref,
    normed_ref, proj_ref, prob_ref, pred_ref, mix_ref,
    embed_ref, all_ref, sems,
):
    token_width = all_ref.shape[0]
    model = normed_ref.shape[1]
    heads, mix, read, end = layout(token_width, model)
    fetches = [
        pltpu.make_async_copy(
            all_hbm.at[:, pl.ds(start, size)], all_ref.at[:, pl.ds(start, size)], sems.at[i]
        )
        for i, (start, size) in enumerate(((0, model), (model, mix - model), (mix, end - mix)))
    ]
    for fetch in fetches:
        fetch.start()
    fetches[0].wait()
    across = (((1,), (1,)), ((), ()))
    embedded = jnp.dot(
        sample_ref[:, :token_width], all_ref[:, :model], preferred_element_type=jnp.float32
    ).astype(jnp.bfloat16)
    embed_ref[...] = embedded
    wide = embedded.astype(jnp.float32)
    mean = jnp.mean(wide, axis=1, keepdims=True)
    removed = wide - mean
    variance = jnp.mean(removed * removed, axis=1, keepdims=True)
    normed = (removed * lax.rsqrt(variance + NORM_EPSILON) * gain_ref[...]).astype(jnp.bfloat16)
    normed_ref[...] = normed
    fetches[1].wait()
    fetches[2].wait()
    mix_ref[...] = all_ref[:, mix:read]
    proj_w = jnp.concatenate(
        [all_ref[:, start : start + heads] for start in range(model, mix, heads)], axis=0
    )
    proj = jnp.dot(normed, proj_w, preferred_element_type=jnp.float32).astype(jnp.bfloat16)
    proj_ref[...] = proj
    attended = []
    for seq in range(sample_ref.shape[0] // SPD):
        rows = slice(seq * SPD, (seq + 1) * SPD)
        parts = []
        for head in range(2):
            query, key, value = (
                proj[rows, i * HD : (i + 1) * HD] for i in range(3 * head, 3 * head + 3)
            )
            scores = lax.dot_general(
                query, key, across, preferred_element_type=jnp.float32
            ) * (1.0 / math.sqrt(HD))
            raised = jnp.exp(scores - jnp.max(scores, axis=-1, keepdims=True))
            probs = raised / jnp.sum(raised, axis=-1, keepdims=True)
            prob_ref[rows, head * SPD : (head + 1) * SPD] = probs
            parts.append(
                jnp.dot(
                    probs.astype(jnp.bfloat16), value, preferred_element_type=jnp.float32
                ).astype(jnp.bfloat16)
            )
        attended.append(jnp.concatenate(parts, axis=1))
    attended = jnp.concatenate(attended, axis=0)
    share = model // 4
    start = pl.multiple_of(chip_ref[0] * share, share)
    pred_ref[...] = jnp.dot(
        jnp.concatenate([attended, attended, embed_ref[:, pl.ds(start, share)]], axis=1),
        jnp.concatenate([all_ref[:, mix:read], all_ref[:share, read:]], axis=0),
        preferred_element_type=jnp.float32,
    ).astype(pred_ref.dtype)


def run_forward(chip, samples, weights, gain):
    rows = samples.shape[0]
    model = gain.shape[1]
    heads = layout(weights.shape[0], model)[0]
    shapes = (
        jax.ShapeDtypeStruct((rows, model), jnp.bfloat16),
        jax.ShapeDtypeStruct((rows, heads), jnp.bfloat16),
        jax.ShapeDtypeStruct((rows, 2 * SPD), jnp.float32),
        jax.ShapeDtypeStruct((rows, HD), jnp.bfloat16),
        jax.ShapeDtypeStruct((weights.shape[0], HD), jnp.bfloat16),
    )
    return pl.pallas_call(
        forward_kernel,
        out_shape=shapes,
        in_specs=[SMEM, VMEM, pl.BlockSpec(memory_space=pl.ANY), VMEM],
        out_specs=(VMEM,) * len(shapes),
        scratch_shapes=[
            pltpu.VMEM((rows, model), jnp.bfloat16),
            pltpu.VMEM(weights.shape, weights.dtype),
            pltpu.SemaphoreType.DMA((3,)),
        ],
        compiler_params=pltpu.CompilerParams(vmem_limit_bytes=FORWARD_LIMIT),
        cost_estimate=pl.CostEstimate(
            flops=2 * rows * model * (weights.shape[0] + heads),
            bytes_accessed=rows * model * 8,
            transcendentals=2 * rows * SPD,
        ),
        name="forward",
    )(chip, samples, weights, gain)


def delta_kernel(share_ref, sample_ref, delta_ref, *, scale):
    targets = sample_ref[:, sample_ref.shape[1] - delta_ref.shape[1] :]
    total = share_ref[0].astype(jnp.float32)
    for i in range(1, share_ref.shape[0]):
        total = total + share_ref[i].astype(jnp.float32)
    delta_ref[...] = ((total - targets.astype(jnp.float32)) * scale).astype(delta_ref.dtype)


def run_delta(shares, samples, scale):
    return pl.pallas_call(
        functools.partial(delta_kernel, scale=scale),
        out_shape=jax.ShapeDtypeStruct(shares.shape[1:], jnp.bfloat16),
        in_specs=[VMEM, VMEM],
        out_specs=VMEM,
        compiler_params=pltpu.CompilerParams(vmem_limit_bytes=LIMIT),
        name="delta",
    )(shares, samples)


def backward_kernel(
    delta_ref, mix_ref, proj_ref, prob_ref, normed_ref, grad_ref, *, head
):
    across = (((1,), (1,)), ((), ()))
    down = (((0,), (0,)), ((), ()))
    delta = delta_ref[...]
    mixing = [mix_ref[(2 * i + head) * HD : (2 * i + head + 1) * HD, :] for i in range(2)]
    grad_attended = lax.dot_general(
        jnp.concatenate([delta, delta], axis=1),
        jnp.concatenate(mixing, axis=1),
        across,
        preferred_element_type=jnp.float32,
    ).astype(jnp.bfloat16)
    grads = []
    for seq in range(delta_ref.shape[0] // SPD):
        rows = slice(seq * SPD, (seq + 1) * SPD)
        query, key, value = (
            proj_ref[rows, i * HD : (i + 1) * HD] for i in range(3 * head, 3 * head + 3)
        )
        upper = grad_attended[rows]
        probs = prob_ref[rows, head * SPD : (head + 1) * SPD]
        grad_probs = lax.dot_general(upper, value, across, preferred_element_type=jnp.float32)
        grad_value = lax.dot_general(
            probs.astype(jnp.bfloat16), upper, down, preferred_element_type=jnp.float32
        )
        inner = jnp.sum(probs * grad_probs, axis=-1, keepdims=True)
        grad_scores = (probs * (grad_probs - inner) * (1.0 / math.sqrt(HD))).astype(jnp.bfloat16)
        grad_query = jnp.dot(grad_scores, key, preferred_element_type=jnp.float32)
        grad_key = lax.dot_general(grad_scores, query, down, preferred_element_type=jnp.float32)
        grads.append(
            jnp.concatenate([grad_query, grad_key, grad_value], axis=1).astype(jnp.bfloat16)
        )
    grads = jnp.concatenate(grads, axis=0)
    total = lax.dot_general(normed_ref[...], grads, down, preferred_element_type=jnp.float32)
    for i in range(grad_ref.shape[0]):
        grad_ref[i] = total[:, i * HD : (i + 1) * HD].astype(grad_ref.dtype)


def run_backward(delta, mix, proj, prob, normed, head):
    rows, model = normed.shape
    heads = proj.shape[1] // 2
    operands = (delta, mix, proj, prob, normed)
    return pl.pallas_call(
        functools.partial(backward_kernel, head=head),
        out_shape=jax.ShapeDtypeStruct((heads // HD, model, HD), jnp.bfloat16),
        in_specs=[VMEM] * len(operands),
        out_specs=VMEM,
        compiler_params=pltpu.CompilerParams(vmem_limit_bytes=LIMIT),
        cost_estimate=pl.CostEstimate(
            flops=2 * rows * model * heads, bytes_accessed=rows * model * 4, transcendentals=0
        ),
        name="backward_other" if head else "backward_own",
    )(*operands)


def sum_over_devices(parts, gain):
    count_x, count_z = lax.axis_size("x"), lax.axis_size("z")
    shape, columns, width = parts.shape, parts.shape[-1], gain.shape[0]
    extra = width // (count_x * columns)

    def exchange(block, values, axis):
        got = swap(jnp.concatenate([block, values.astype(jnp.bfloat16)], axis=1), axis)
        return (
            jnp.sum(got[:, :-extra].astype(jnp.float32), axis=0).astype(jnp.bfloat16),
            jnp.sum(got[:, -extra:].astype(jnp.float32), axis=0),
        )

    part, gain = exchange(
        parts.reshape(count_x, -1, columns), gain.reshape(count_x, extra, columns), "x"
    )
    total, gain = exchange(
        part.reshape(count_z, -1, columns),
        jnp.broadcast_to(gain, (count_z, extra, columns)),
        "z",
    )
    got = spread(total, "z").reshape(-1, columns)
    for axis in ("core", "grp", "yhi"):
        gain = gain + swap_with(gain, axis)
    sent = jnp.concatenate([got, gain.astype(jnp.bfloat16)], axis=0)
    got = spread(sent, "x").reshape(count_x, -1, columns)
    gain = got[:, -extra:].astype(jnp.float32)
    return got[:, :-extra].reshape(shape), gain.reshape(width)


def shards(
    start_field,
    material,
    conductivity,
    owners,
    tile_ids,
    embed_weight,
    layer_norm_gain,
    w_qkv,
    w_out,
    w_read,
):
    gain_row = layer_norm_gain[None, :]
    final_local, send, place, embed = run_slab(
        start_field[0],
        material,
        conductivity[0],
        owners[0, 0, :, :, 0],
        tile_ids[0, 0],
        embed_weight.T,
    )
    send, embed = lax.optimization_barrier((send, embed))
    got = swap(send.reshape(lax.axis_size(SPACE), -1, send.shape[1]), SPACE)
    embed = jnp.stack([embed, swap_with(embed, "grp")])
    embed, w_own, out_own = lax.optimization_barrier((embed, w_qkv, w_out))
    w_other, out_other = swap_cores(w_own), swap_cores(out_own)
    embed = jnp.stack([embed, swap_cores(embed)]).reshape((-1,) + embed_weight.T.shape)
    away = lax.axis_index(GROUP) ^ jnp.arange(embed.shape[0], dtype=jnp.int32)
    order = ((away & 1) << 2) + ((away >> 2 & 1) << 1) + (away >> 1 & 1)

    chip = lax.axis_index(CHIPS).astype(jnp.int32)[None]
    order = jnp.concatenate([order, chip])
    weights = run_prepare(order, embed, w_own, w_other, out_own, out_other, w_read)
    got, weights, gain_row = lax.optimization_barrier((got, weights, gain_row))
    got = got.reshape(-1, got.shape[2])

    chips = lax.axis_size(CHIPS)
    copies = jnp.dot(
        jnp.tile(place, (chips, 1)), got, preferred_element_type=jnp.float32
    ).astype(jnp.bfloat16)
    samples = swap(copies, CHIPS)

    normed, proj, prob, pred, mix = run_forward(chip, samples, weights, gain_row)
    shares = spread(pred, CHIPS).reshape((chips,) + pred.shape)
    row_count = lax.axis_size(GROUP) * SPD
    loss_scale = math.sqrt(
        w_read.shape[0] / (lax.axis_size(SPACE) * row_count * w_read.shape[1])
    )
    delta = run_delta(shares, samples, loss_scale)

    saved = (mix, proj, prob, normed)
    grads_other = swap_cores(run_backward(delta, *saved, head=1))
    grads = (
        run_backward(delta, *saved, head=0).astype(jnp.float32) + grads_other.astype(jnp.float32)
    ).astype(jnp.bfloat16)

    gain_share = (
        jnp.sum(w_qkv.astype(jnp.float32) * grads.astype(jnp.float32), axis=(0, 2))
        / layer_norm_gain
    )
    weight_total, gain_total = sum_over_devices(grads, gain_share)
    return (final_local[None], weight_total, gain_total)


def solution(mesh):
    halves, space, members = (mesh.shape[name] for name in ("grp", "space", "mem"))
    fine = Mesh(
        mesh.devices.reshape(halves, space // 4, 4, members // 2, 2),
        ("grp", "z", "x", "yhi", "core"),
    )
    placed = (
        P(MEM, SPACE, "grp", None),
        P(SPACE, "grp", None),
        P(MEM, None),
        P(MEM, "grp", None, None, None),
        P(MEM, "grp", None, None),
        P(None, GROUP),
        P(),
        P(None, None, GROUP),
        P(GROUP, None),
        P(),
    )
    return jax.shard_map(
        shards,
        mesh=fine,
        in_specs=placed,
        out_specs=(P(MEM, SPACE, "grp", None), P(None, None, GROUP), P()),
        check_vma=False,
    )
```

```python
import functools
import math

import jax
import jax.numpy as jnp
from jax import lax
from jax.experimental import pallas as pl
from jax.experimental.pallas import tpu as pltpu
from jax.sharding import Mesh
from jax.sharding import PartitionSpec as P

SPD = 128
STEPS = 3
TILE = 16
HD = 128
NORM_EPSILON = 1e-06

SPACE = ("z", "x")
MEM = ("yhi", "core")
GROUP = ("grp", "yhi", "core")
CHIPS = ("grp", "yhi")

PAD = 4
VMEM = pl.BlockSpec(memory_space=pltpu.VMEM)
SMEM = pl.BlockSpec(memory_space=pltpu.SMEM)
LIMIT = 20 * 1024 * 1024
FORWARD_LIMIT = 48 * 1024 * 1024
EXACT = lax.Precision.HIGHEST


def swap(parts, axis):
    return lax.all_to_all(parts, axis, split_axis=0, concat_axis=0, tiled=True)


def spread(own, axis):
    count = lax.axis_size(axis)
    return swap(jnp.broadcast_to(own[None], (count,) + own.shape), axis)


def swap_with(own, axis):
    return lax.ppermute(own, axis, [(0, 1), (1, 0)])


def swap_cores(own):
    return swap_with(own, "core")


def halos(field, material, width, beside):
    half = lax.axis_index("grp")

    def cut(span, axis):
        return jnp.stack(
            [
                lax.slice_in_dim(field, *span, axis=axis),
                lax.slice_in_dim(material, *span, axis=axis).astype(jnp.float32),
            ]
        )

    span_x, span_y = field.shape[:2]
    face = jnp.where(
        half == 0, cut((span_y - width, span_y), 1), cut((0, width), 1)
    )
    side = swap_with(face, "grp")
    side, beside = lax.optimization_barrier((side, beside))
    count = lax.axis_size(SPACE)
    forward = [(i, i + 1) for i in range(count - 1)]
    backward = [(i + 1, i) for i in range(count - 1)]
    top, bottom = side[:, -width:], side[:, :width]
    top = jnp.concatenate([top, cut((span_x - width, span_x), 0), top], axis=2)
    bottom = jnp.concatenate([bottom, cut((0, width), 0), bottom], axis=2)
    low = lax.ppermute(top, SPACE, forward)
    high = lax.ppermute(bottom, SPACE, backward)
    return side, low, high, beside


def over(first, last, body):
    for plane in range(first, last):
        body(plane)


def slab_kernel(
    place_ref,
    table_ref,
    field_ref,
    material_ref,
    side_ref,
    low_ref,
    high_ref,
    pick_ref,
    final_ref,
    send_ref,
    field_a,
    field_b,
    cond,
    coef,
    pairs,
    quads,
    rows_t,
    *,
    total_x,
    total_y,
):
    span_x, span_y, span_z = field_ref.shape
    width = low_ref.shape[1]
    rows = span_y + 2 * PAD
    planes = span_x + 2 * width
    own_x = slice(width, width + span_x)
    own_y = slice(PAD, PAD + span_y)
    ext_y = slice(PAD - width, PAD + span_y + width)

    field_a[...] = jnp.zeros_like(field_a)
    cond[...] = jnp.zeros_like(cond)
    for part, target in ((0, field_a), (1, cond)):
        target[own_x, slice(PAD - width, PAD), :] = side_ref[part]
        target[own_x, slice(PAD + span_y, PAD + span_y + width), :] = side_ref[part]
        target[slice(0, width), ext_y, :] = low_ref[part]
        target[slice(width + span_x, planes), ext_y, :] = high_ref[part]
    field_a[own_x, own_y, :] = field_ref[...]
    cond[own_x, own_y, :] = material_ref[...].astype(jnp.float32)

    place_x = place_ref[0] * span_x - width
    place_y = place_ref[1] * span_y - PAD
    row_id = place_y + lax.broadcasted_iota(jnp.int32, (rows, span_z), 0)
    col_id = lax.broadcasted_iota(jnp.int32, (rows, span_z), 1)
    inside_y = (row_id >= 0) & (row_id < total_y)
    first_z = col_id == 0
    last_z = col_id == span_z - 1

    def inside(plane):
        at = place_x + plane
        in_x = ((at >= 0) & (at < total_x)).astype(jnp.int32)
        return inside_y & (jnp.full((rows, span_z), in_x) > 0)

    def set_cond(plane):
        kind = cond[plane]
        value = jnp.zeros_like(kind)
        for level in range(table_ref.shape[0]):
            value = jnp.where(kind == float(level), table_ref[level], value)
        keep = inside(plane)
        cond[plane] = jnp.where(keep, value, 0.0)
        field_a[plane] = jnp.where(keep, field_a[plane], 0.0)

    over(0, planes, set_cond)

    def set_coef(plane):
        mine = 0.5 * cond[plane]
        keep = inside(plane)
        ups = mine + pltpu.roll(mine, 1, 0)
        downs = mine + pltpu.roll(mine, rows - 1, 0)
        before = mine + jnp.where(first_z, 0.0, pltpu.roll(mine, 1, 1))
        after = mine + jnp.where(last_z, 0.0, pltpu.roll(mine, span_z - 1, 1))
        left = mine + 0.5 * cond[plane - 1]
        right = mine + 0.5 * cond[plane + 1]
        rest = 1.0 - (ups + downs + before + after + left + right)
        coef[0, plane] = jnp.where(keep, rest, 0.0)
        coef[1, plane] = jnp.where(keep, left, 0.0)
        coef[2, plane] = jnp.where(keep, right, 0.0)
        coef[3, plane] = jnp.where(keep, ups, 0.0)
        coef[4, plane] = jnp.where(keep, downs, 0.0)
        coef[5, plane] = jnp.where(keep & ~first_z, before, 0.0)
        coef[6, plane] = jnp.where(keep & ~last_z, after, 0.0)

    over(1, planes - 1, set_coef)

    def step(source, target):
        def one(plane):
            mid = source[plane]
            value = coef[0, plane] * mid
            value = value + coef[1, plane] * source[plane - 1]
            value = value + coef[2, plane] * source[plane + 1]
            value = value + coef[3, plane] * pltpu.roll(mid, 1, 0)
            value = value + coef[4, plane] * pltpu.roll(mid, rows - 1, 0)
            value = value + coef[5, plane] * pltpu.roll(mid, 1, 1)
            value = value + coef[6, plane] * pltpu.roll(mid, span_z - 1, 1)
            target[plane] = value

        return one

    for number in range(STEPS):
        source, target = (field_a, field_b) if number % 2 == 0 else (field_b, field_a)
        over(1 + number, planes - 1 - number, step(source, target))

    before_last, last = (field_a, field_b) if STEPS % 2 == 1 else (field_b, field_a)
    final_ref[...] = last[own_x, own_y, :]

    for i in range(span_x // 2):
        plane = width + 2 * i
        pairs[span_y * i : span_y * (i + 1), :] = (
            before_last[plane, own_y, :] + before_last[plane + 1, own_y, :]
        )
    for i in range(span_x // 4):
        plane = width + 4 * i
        quads[span_y * i : span_y * (i + 1), :] = (
            last[plane, own_y, :] + last[plane + 1, own_y, :]
        ) + (last[plane + 2, own_y, :] + last[plane + 3, own_y, :])
    depth = TILE // 2
    tiles = span_z // TILE
    z_id = lax.broadcasted_iota(jnp.int32, (span_z, depth * tiles), 0) // 2
    c_id = lax.broadcasted_iota(jnp.int32, (span_z, depth * tiles), 1)
    fold_z = (z_id == (c_id % tiles) * depth + c_id // tiles).astype(jnp.float32)

    def fold_y(stacked, group):
        size = stacked.shape[0]
        out_id = lax.broadcasted_iota(jnp.int32, (size // group, size), 0)
        in_id = lax.broadcasted_iota(jnp.int32, (size // group, size), 1)
        matrix = (out_id == in_id // group).astype(jnp.float32)
        part = jnp.dot(stacked, fold_z, precision=EXACT, preferred_element_type=jnp.float32)
        return jnp.dot(matrix, part, precision=EXACT, preferred_element_type=jnp.float32)

    fine = fold_y(pairs[...], 2) * 0.125
    rough = fold_y(quads[...], 4) * 0.03125
    fine_rows, rough_rows = fine.shape[0], rough.shape[0]
    for k in range(depth):
        cut = slice(tiles * k, tiles * (k + 1))
        rows_t[pl.ds(k, fine_rows, stride=depth), :] = fine[:, cut]
        rows_t[pl.ds(fine_rows * depth + k, rough_rows, stride=depth), :] = rough[:, cut]
    send_ref[...] = lax.dot_general(
        pick_ref[...],
        rows_t[...].astype(jnp.bfloat16),
        (((1,), (1,)), ((), ())),
        preferred_element_type=jnp.float32,
    ).astype(jnp.bfloat16)


def run_slab(field, material, table, owner_list, tile_list, embed_own):
    pick, place = slots(owner_list, tile_list, field.shape[2] // TILE)
    side, low, high, embed_own = halos(field, material, STEPS, embed_own)
    embed = jnp.stack([embed_own, swap_with(embed_own, "yhi")])
    origin = jnp.stack([lax.axis_index(SPACE), lax.axis_index("grp")]).astype(jnp.int32)
    totals = (lax.axis_size(SPACE) * field.shape[0], lax.axis_size("grp") * field.shape[1])
    final, send = call_slab(origin, table, field, material, side, low, high, pick, totals)
    return final, send, place, embed


def call_slab(origin, table, field, material, side, low, high, pick, totals):
    span_x, span_y, span_z = field.shape
    planes, rows = span_x + 2 * low.shape[1], span_y + 2 * PAD
    tiles = span_z // TILE
    values = (span_x * span_y // 4 + span_x * span_y // 16) * TILE // 2
    extended = pltpu.VMEM((planes, rows, span_z), jnp.float32)
    return pl.pallas_call(
        functools.partial(slab_kernel, total_x=totals[0], total_y=totals[1]),
        out_shape=(
            jax.ShapeDtypeStruct(field.shape, jnp.float32),
            jax.ShapeDtypeStruct((pick.shape[0], values), jnp.bfloat16),
        ),
        in_specs=[SMEM, SMEM] + [VMEM] * 6,
        out_specs=(VMEM, VMEM),
        scratch_shapes=[
            extended,
            extended,
            extended,
            pltpu.VMEM((7, planes, rows, span_z), jnp.float32),
            pltpu.VMEM((span_x * span_y // 2, span_z), jnp.float32),
            pltpu.VMEM((span_x * span_y // 4, span_z), jnp.float32),
            pltpu.VMEM((values, tiles), jnp.float32),
        ],
        compiler_params=pltpu.CompilerParams(vmem_limit_bytes=LIMIT),
        name="slab",
    )(origin, table, field, material, side, low, high, pick)


def slots(owner_list, tile_list, tile_count):
    shard_count, slot_count = owner_list.shape
    capacity = 2 * slot_count // shard_count
    my_index = lax.axis_index(SPACE)
    slot_order = jnp.arange(slot_count, dtype=jnp.int32)
    earlier = slot_order[:, None] < slot_order[None, :]
    owned_here = owner_list == my_index
    here_rank = jnp.dot(
        owned_here.astype(jnp.bfloat16),
        earlier.astype(jnp.bfloat16),
        preferred_element_type=jnp.float32,
    ).astype(jnp.int32)
    slot_ids = jnp.arange(capacity, dtype=jnp.int32)
    slot_match = owned_here[:, None, :] & (here_rank[:, None, :] == slot_ids[None, :, None])
    chosen = jnp.sum(jnp.where(slot_match, tile_list[:, None, :] + 1, 0), axis=2) - 1
    tile_ids = jnp.arange(tile_count, dtype=jnp.int32)
    pick = (chosen.reshape(-1, 1) == tile_ids[None, :]).astype(jnp.bfloat16)
    own_owner = jnp.take(owner_list, my_index, axis=0)
    same_owner = own_owner[:, None] == own_owner[None, :]
    own_rank = jnp.sum((same_owner & earlier).astype(jnp.int32), axis=0)
    flat_index = own_owner * capacity + own_rank
    flat_ids = jnp.arange(shard_count * capacity, dtype=jnp.int32)
    place = (flat_index[:, None] == flat_ids[None, :]).astype(jnp.bfloat16)
    return pick, place


def layout(token_width, model):
    heads = 6 * HD
    mix = model + model // token_width * heads
    return heads, mix, mix + HD, mix + 2 * HD


def prepare_kernel(
    order_ref, parts_ref, w_own_ref, w_other_ref, out_own_ref, out_other_ref, read_ref, all_ref
):
    count, width, rows = parts_ref.shape
    model = count * width
    heads, mix, read, _ = layout(rows, model)
    for i in range(count // 2):
        pair = jnp.concatenate(
            [parts_ref[order_ref[2 * i]], parts_ref[order_ref[2 * i + 1]]], axis=0
        )
        all_ref[:, 2 * i * width : 2 * (i + 1) * width] = pair.T
    for block in range(model // rows):
        for head, ref in enumerate((w_own_ref, w_other_ref)):
            for i in range(3):
                start = model + block * heads + (3 * head + i) * HD
                all_ref[:, start : start + HD] = ref[i, block * rows : (block + 1) * rows, :]
    out_w = jnp.concatenate([out_own_ref[...], out_other_ref[...]], axis=0)
    mixing = jnp.dot(out_w, read_ref[...], preferred_element_type=jnp.float32)
    high = mixing.astype(jnp.bfloat16)
    all_ref[: 2 * HD, mix:read] = high
    all_ref[2 * HD :, mix:read] = (mixing - high.astype(jnp.float32)).astype(jnp.bfloat16)
    share = 2 * width
    start = pl.multiple_of(order_ref[count] * share, share)
    all_ref[:share, read:] = read_ref[pl.ds(start, share), :]
    all_ref[share:, read:] = jnp.zeros((rows - share, HD), jnp.bfloat16)


def run_prepare(order, parts, w_own, w_other, out_own, out_other, w_read):
    rows, model = parts.shape[2], w_own.shape[1]
    return pl.pallas_call(
        prepare_kernel,
        out_shape=jax.ShapeDtypeStruct((rows, layout(rows, model)[-1]), jnp.bfloat16),
        in_specs=[SMEM] + [VMEM] * 6,
        out_specs=VMEM,
        compiler_params=pltpu.CompilerParams(vmem_limit_bytes=LIMIT),
        cost_estimate=pl.CostEstimate(flops=1 << 28, bytes_accessed=1 << 23, transcendentals=0),
        name="prepare",
    )(order, parts, w_own, w_other, out_own, out_other, w_read)


def forward_kernel(
    chip_ref, sample_ref, all_hbm, gain_ref,
    normed_ref, proj_ref, prob_ref, pred_ref, mix_ref,
    embed_ref, all_ref, sems,
):
    token_width = all_ref.shape[0]
    model = normed_ref.shape[1]
    heads, mix, read, end = layout(token_width, model)
    fetches = [
        pltpu.make_async_copy(
            all_hbm.at[:, pl.ds(start, size)], all_ref.at[:, pl.ds(start, size)], sems.at[i]
        )
        for i, (start, size) in enumerate(
            [(part * model // 3, model // 3) for part in range(3)]
            + [(model, mix - model), (mix, end - mix)]
        )
    ]
    for fetch in fetches[:3]:
        fetch.start()
    across = (((1,), (1,)), ((), ()))
    tokens = sample_ref[:, :token_width]
    parts = []
    for part in range(3):
        columns = slice(part * model // 3, (part + 1) * model // 3)
        fetches[part].wait()
        if part == 2:
            for fetch in fetches[3:]:
                fetch.start()
        parts.append(
            jnp.dot(tokens, all_ref[:, columns], preferred_element_type=jnp.float32).astype(
                jnp.bfloat16
            )
        )
    embedded = jnp.concatenate(parts, axis=1)
    embed_ref[...] = embedded
    wide = embedded.astype(jnp.float32)
    mean = jnp.mean(wide, axis=1, keepdims=True)
    removed = wide - mean
    variance = jnp.mean(removed * removed, axis=1, keepdims=True)
    normed = (removed * lax.rsqrt(variance + NORM_EPSILON) * gain_ref[...]).astype(jnp.bfloat16)
    normed_ref[...] = normed
    for fetch in fetches[3:]:
        fetch.wait()
    mix_ref[...] = all_ref[:, mix:read]
    proj_w = jnp.concatenate(
        [all_ref[:, start : start + heads] for start in range(model, mix, heads)], axis=0
    )
    proj = jnp.dot(normed, proj_w, preferred_element_type=jnp.float32).astype(jnp.bfloat16)
    proj_ref[...] = proj
    attended = []
    for seq in range(sample_ref.shape[0] // SPD):
        rows = slice(seq * SPD, (seq + 1) * SPD)
        parts = []
        for head in range(2):
            query, key, value = (
                proj[rows, i * HD : (i + 1) * HD] for i in range(3 * head, 3 * head + 3)
            )
            scores = lax.dot_general(
                query, key, across, preferred_element_type=jnp.float32
            ) * (1.0 / math.sqrt(HD))
            raised = jnp.exp(scores - jnp.max(scores, axis=-1, keepdims=True))
            probs = raised / jnp.sum(raised, axis=-1, keepdims=True)
            prob_ref[rows, head * SPD : (head + 1) * SPD] = probs
            parts.append(
                jnp.dot(
                    probs.astype(jnp.bfloat16), value, preferred_element_type=jnp.float32
                ).astype(jnp.bfloat16)
            )
        attended.append(jnp.concatenate(parts, axis=1))
    attended = jnp.concatenate(attended, axis=0)
    share = model // 4
    start = pl.multiple_of(chip_ref[0] * share, share)
    pred_ref[...] = jnp.dot(
        jnp.concatenate([attended, attended, embed_ref[:, pl.ds(start, share)]], axis=1),
        jnp.concatenate([all_ref[:, mix:read], all_ref[:share, read:]], axis=0),
        preferred_element_type=jnp.float32,
    ).astype(pred_ref.dtype)


def run_forward(chip, samples, weights, gain):
    rows = samples.shape[0]
    model = gain.shape[1]
    heads = layout(weights.shape[0], model)[0]
    shapes = (
        jax.ShapeDtypeStruct((rows, model), jnp.bfloat16),
        jax.ShapeDtypeStruct((rows, heads), jnp.bfloat16),
        jax.ShapeDtypeStruct((rows, 2 * SPD), jnp.float32),
        jax.ShapeDtypeStruct((rows, HD), jnp.bfloat16),
        jax.ShapeDtypeStruct((weights.shape[0], HD), jnp.bfloat16),
    )
    return pl.pallas_call(
        forward_kernel,
        out_shape=shapes,
        in_specs=[SMEM, VMEM, pl.BlockSpec(memory_space=pl.ANY), VMEM],
        out_specs=(VMEM,) * len(shapes),
        scratch_shapes=[
            pltpu.VMEM((rows, model), jnp.bfloat16),
            pltpu.VMEM(weights.shape, weights.dtype),
            pltpu.SemaphoreType.DMA((5,)),
        ],
        compiler_params=pltpu.CompilerParams(vmem_limit_bytes=FORWARD_LIMIT),
        cost_estimate=pl.CostEstimate(
            flops=2 * rows * model * (weights.shape[0] + heads),
            bytes_accessed=rows * model * 8,
            transcendentals=2 * rows * SPD,
        ),
        name="forward",
    )(chip, samples, weights, gain)


def delta_kernel(share_ref, sample_ref, delta_ref, *, scale):
    targets = sample_ref[:, sample_ref.shape[1] - delta_ref.shape[1] :]
    total = share_ref[0].astype(jnp.float32)
    for i in range(1, share_ref.shape[0]):
        total = total + share_ref[i].astype(jnp.float32)
    delta_ref[...] = ((total - targets.astype(jnp.float32)) * scale).astype(delta_ref.dtype)


def run_delta(shares, samples, scale):
    return pl.pallas_call(
        functools.partial(delta_kernel, scale=scale),
        out_shape=jax.ShapeDtypeStruct(shares.shape[1:], jnp.bfloat16),
        in_specs=[VMEM, VMEM],
        out_specs=VMEM,
        compiler_params=pltpu.CompilerParams(vmem_limit_bytes=LIMIT),
        name="delta",
    )(shares, samples)


def backward_kernel(
    delta_ref, mix_ref, proj_ref, prob_ref, normed_ref, grad_ref, *, head
):
    across = (((1,), (1,)), ((), ()))
    down = (((0,), (0,)), ((), ()))
    delta = delta_ref[...]
    mixing = [mix_ref[(2 * i + head) * HD : (2 * i + head + 1) * HD, :] for i in range(2)]
    grad_attended = lax.dot_general(
        jnp.concatenate([delta, delta], axis=1),
        jnp.concatenate(mixing, axis=1),
        across,
        preferred_element_type=jnp.float32,
    ).astype(jnp.bfloat16)
    grads = []
    for seq in range(delta_ref.shape[0] // SPD):
        rows = slice(seq * SPD, (seq + 1) * SPD)
        query, key, value = (
            proj_ref[rows, i * HD : (i + 1) * HD] for i in range(3 * head, 3 * head + 3)
        )
        upper = grad_attended[rows]
        probs = prob_ref[rows, head * SPD : (head + 1) * SPD]
        grad_probs = lax.dot_general(upper, value, across, preferred_element_type=jnp.float32)
        grad_value = lax.dot_general(
            probs.astype(jnp.bfloat16), upper, down, preferred_element_type=jnp.float32
        )
        inner = jnp.sum(probs * grad_probs, axis=-1, keepdims=True)
        grad_scores = (probs * (grad_probs - inner) * (1.0 / math.sqrt(HD))).astype(jnp.bfloat16)
        grad_query = jnp.dot(grad_scores, key, preferred_element_type=jnp.float32)
        grad_key = lax.dot_general(grad_scores, query, down, preferred_element_type=jnp.float32)
        grads.append(
            jnp.concatenate([grad_query, grad_key, grad_value], axis=1).astype(jnp.bfloat16)
        )
    grads = jnp.concatenate(grads, axis=0)
    total = lax.dot_general(normed_ref[...], grads, down, preferred_element_type=jnp.float32)
    for i in range(grad_ref.shape[0]):
        grad_ref[i] = total[:, i * HD : (i + 1) * HD].astype(grad_ref.dtype)


def run_backward(delta, mix, proj, prob, normed, head):
    rows, model = normed.shape
    heads = proj.shape[1] // 2
    operands = (delta, mix, proj, prob, normed)
    return pl.pallas_call(
        functools.partial(backward_kernel, head=head),
        out_shape=jax.ShapeDtypeStruct((heads // HD, model, HD), jnp.bfloat16),
        in_specs=[VMEM] * len(operands),
        out_specs=VMEM,
        compiler_params=pltpu.CompilerParams(vmem_limit_bytes=LIMIT),
        cost_estimate=pl.CostEstimate(
            flops=2 * rows * model * heads, bytes_accessed=rows * model * 4, transcendentals=0
        ),
        name="backward_other" if head else "backward_own",
    )(*operands)


def sum_over_devices(parts, gain):
    count_x, count_z = lax.axis_size("x"), lax.axis_size("z")
    shape, columns, width = parts.shape, parts.shape[-1], gain.shape[0]
    extra = width // (count_x * columns)

    def exchange(block, values, axis):
        got = swap(jnp.concatenate([block, values.astype(jnp.bfloat16)], axis=1), axis)
        return (
            jnp.sum(got[:, :-extra].astype(jnp.float32), axis=0).astype(jnp.bfloat16),
            jnp.sum(got[:, -extra:].astype(jnp.float32), axis=0),
        )

    part, gain = exchange(
        parts.reshape(count_x, -1, columns), gain.reshape(count_x, extra, columns), "x"
    )
    total, gain = exchange(
        part.reshape(count_z, -1, columns),
        jnp.broadcast_to(gain, (count_z, extra, columns)),
        "z",
    )
    got = spread(total, "z").reshape(-1, columns)
    for axis in ("core", "grp", "yhi"):
        gain = gain + swap_with(gain, axis)
    sent = jnp.concatenate([got, gain.astype(jnp.bfloat16)], axis=0)
    got = spread(sent, "x").reshape(count_x, -1, columns)
    gain = got[:, -extra:].astype(jnp.float32)
    return got[:, :-extra].reshape(shape), gain.reshape(width)


def shards(
    start_field,
    material,
    conductivity,
    owners,
    tile_ids,
    embed_weight,
    layer_norm_gain,
    w_qkv,
    w_out,
    w_read,
):
    gain_row = layer_norm_gain[None, :]
    final_local, send, place, embed = run_slab(
        start_field[0],
        material,
        conductivity[0],
        owners[0, 0, :, :, 0],
        tile_ids[0, 0],
        embed_weight.T,
    )
    send, embed = lax.optimization_barrier((send, embed))
    got = swap(send.reshape(lax.axis_size(SPACE), -1, send.shape[1]), SPACE)
    embed = jnp.stack([embed, swap_with(embed, "grp")])
    embed, w_own, out_own = lax.optimization_barrier((embed, w_qkv, w_out))
    w_other, out_other = swap_cores(w_own), swap_cores(out_own)
    embed = jnp.stack([embed, swap_cores(embed)]).reshape((-1,) + embed_weight.T.shape)
    away = lax.axis_index(GROUP) ^ jnp.arange(embed.shape[0], dtype=jnp.int32)
    order = ((away & 1) << 2) + ((away >> 2 & 1) << 1) + (away >> 1 & 1)

    chip = lax.axis_index(CHIPS).astype(jnp.int32)[None]
    order = jnp.concatenate([order, chip])
    weights = run_prepare(order, embed, w_own, w_other, out_own, out_other, w_read)
    got, weights, gain_row = lax.optimization_barrier((got, weights, gain_row))
    got = got.reshape(-1, got.shape[2])

    chips = lax.axis_size(CHIPS)
    copies = jnp.dot(
        jnp.tile(place, (chips, 1)), got, preferred_element_type=jnp.float32
    ).astype(jnp.bfloat16)
    samples = swap(copies, CHIPS)

    normed, proj, prob, pred, mix = run_forward(chip, samples, weights, gain_row)
    shares = spread(pred, CHIPS).reshape((chips,) + pred.shape)
    row_count = lax.axis_size(GROUP) * SPD
    loss_scale = math.sqrt(
        w_read.shape[0] / (lax.axis_size(SPACE) * row_count * w_read.shape[1])
    )
    delta = run_delta(shares, samples, loss_scale)

    saved = (mix, proj, prob, normed)
    grads_other = swap_cores(run_backward(delta, *saved, head=1))
    grads = (
        run_backward(delta, *saved, head=0).astype(jnp.float32) + grads_other.astype(jnp.float32)
    ).astype(jnp.bfloat16)

    gain_share = (
        jnp.sum(w_qkv.astype(jnp.float32) * grads.astype(jnp.float32), axis=(0, 2))
        / layer_norm_gain
    )
    weight_total, gain_total = sum_over_devices(grads, gain_share)
    return (final_local[None], weight_total, gain_total)


def solution(mesh):
    halves, space, members = (mesh.shape[name] for name in ("grp", "space", "mem"))
    fine = Mesh(
        mesh.devices.reshape(halves, space // 4, 4, members // 2, 2),
        ("grp", "z", "x", "yhi", "core"),
    )
    placed = (
        P(MEM, SPACE, "grp", None),
        P(SPACE, "grp", None),
        P(MEM, None),
        P(MEM, "grp", None, None, None),
        P(MEM, "grp", None, None),
        P(None, GROUP),
        P(),
        P(None, None, GROUP),
        P(GROUP, None),
        P(),
    )
    return jax.shard_map(
        shards,
        mesh=fine,
        in_specs=placed,
        out_specs=(P(MEM, SPACE, "grp", None), P(None, None, GROUP), P()),
        check_vma=False,
    )
```
